32 devices in a mesh: groups: 2 (over y), sec: 4 (over z), tile: 2 (over x), row: 2 (over core).
Axes of the slice: x: 2, y: 2, z: 4, core: 2. Of those that a mesh axis runs over, the one named last changes fastest.
Arguments:
- section_pixels: float32 [8, 512, 4096], P(('groups', 'sec'), ('tile', 'row')), parts along dimension 0, may hold values from -40 to 40
- jitter_index: int32 [8, 512], P(('groups', 'sec'), ('tile', 'row')), parts along dimension 0, may hold values from 0 to 7
- drift_list: int32 [8, 4, 8, 3], P(('groups', 'sec')), parts along dimension 0, may hold values from 0 to 31, as said below
- blend_weight: float32 [8, 4, 8], P(('groups', 'sec')), parts along dimension 0, may hold values from 0.5 to 2
- patch_col: int32 [4, 8], P(('tile', 'row'), 'groups'), parts along dimension 1, may hold values from 0 to 896
Outputs:
- jitter_phase: float32 [8, 512], P(('groups', 'sec'), ('tile', 'row')), parts along dimension 0
- surfaces: float32 [6, 4, 4, 128, 128], P('groups', ('tile', 'row'), 'sec'), parts along dimension 0
The draws below stay inside these ranges and needn't reach their ends.
There are 2 independent parts, one for each index of `groups`. The reference program is written for one: setup_inputs(seed, part) draws one part's arguments, and reference() takes and returns one part's arrays. A program takes and returns all parts, laid end to end along the dimension named above; each array names one. Nothing has to cross between parts.
Inputs may be any that keep to these rules, and one draw needn't show every extreme that they name: `drift_list`: entry [s, j, k] names a block of band j (distinct over k), the band that owns its target, and the target block. No band sends more than 2 blocks to one owner, and in every section one owner receives exactly 2 blocks from every band.
All inputs are finite; a program needn't handle non-finite values.
Results may differ from the reference program's by a relative error of at most 0.0065.
Values may be sent and summed in bfloat16 or wider, within the bound.
No kernel may reach another device: no remote copies, remote signals or barrier semaphores. Data moves between devices by JAX's collectives and lax.ppermute only.
A program may use at most 64 MiB of HBM per device.

```python
import math
import jax
import jax.numpy as jnp
from jax import lax

W = 4096
SEG = 512
PATCH = 128
BLOCK = 128
JMAX = 8
OV = 8
CAP = 2
ROWS_DEV = 128
SECTIONS = 4
OWNERS = 4
ROWS = 512
NBLK = 32
N_SEC = 4


def coarse_delays(key):
    return jax.random.randint(jax.random.fold_in(key, 11), (SECTIONS, ROWS), 0, JMAX).astype(jnp.int32)


def draw_jitter_index(key, part):
    return coarse_delays(key)


def draw_section_pixels(key, part):
    delays = coarse_delays(key)
    span_cols = W + JMAX + 1
    shared = jax.random.normal(jax.random.fold_in(key, 21), (1, ROWS + 1, span_cols), jnp.float32)
    own_field = jax.random.normal(jax.random.fold_in(key, 22), (SECTIONS, ROWS + 1, span_cols), jnp.float32)
    field_sum = 0.3 * shared + own_field
    mixed = (field_sum[:, 1:] + field_sum[:, :-1]) * 0.7071
    fraction = jax.random.uniform(jax.random.fold_in(key, 23), (SECTIONS, ROWS, 1), jnp.float32)
    columns = jnp.arange(W, dtype=jnp.int32)[None, None, :] - delays[:, :, None] + JMAX
    first_pick = jnp.take_along_axis(mixed, columns, 2)
    second_pick = jnp.take_along_axis(mixed, columns + 1, 2)
    noise_part = jax.random.normal(jax.random.fold_in(key, 24), (SECTIONS, ROWS, W), jnp.float32)
    picture = (1.0 - fraction) * first_pick + fraction * second_pick + 0.3 * noise_part
    return jnp.clip(picture, -40.0, 40.0)


def draw_drift_list(key, part):
    slot_count = OWNERS * CAP

    def one_band(band_key, hot_owner):
        perm_key, source_key, target_key, order_key = jax.random.split(band_key, 4)
        ordering = jax.random.permutation(perm_key, slot_count)
        placing = jnp.argsort(ordering)
        slot_ids = jnp.arange(slot_count, dtype=jnp.int32)
        sort_keys = jnp.where(slot_ids // CAP == hot_owner, slot_ids % CAP - CAP, placing)
        chosen = jnp.argsort(sort_keys)[:OV]
        owner_ids = chosen // CAP
        source_ids = jax.random.permutation(source_key, NBLK)[:OV]
        target_ids = jax.random.randint(target_key, (OV,), 0, NBLK)
        listing = jnp.stack([source_ids, owner_ids, target_ids], 1)
        return listing[jax.random.permutation(order_key, OV)]

    def one_section(section_key):
        hot_owner = jax.random.randint(jax.random.fold_in(section_key, 1), (), 0, OWNERS)
        band_keys = jax.random.split(jax.random.fold_in(section_key, 2), OWNERS)
        return jax.vmap(one_band, in_axes=(0, None))(band_keys, hot_owner)
    section_keys = jax.random.split(jax.random.fold_in(key, 31), SECTIONS)
    return jax.vmap(one_section)(section_keys).astype(jnp.int32)


def with_ends(result, own_key, smallest, high):
    shape = result.shape
    index_at = [jax.random.randint(jax.random.fold_in(own_key, axis), (), 0, shape[axis]) for axis in range(len(shape))]
    result = result.at[tuple(index_at)].set(smallest)
    longest = shape.index(max(shape))
    index_at[longest] = (index_at[longest] + 1) % shape[longest]
    return result.at[tuple(index_at)].set(high)


def block_levels(stream_key, extent, cuts, smallest, top_value):
    loudness, own = 1.0, jax.random.fold_in(stream_key, 6)
    for axis_at, shards_of in cuts:
        heights = jnp.exp(jax.random.uniform(jax.random.fold_in(own, axis_at), (shards_of,), jnp.float32, smallest / len(cuts), top_value / len(cuts)))
        loudness = loudness * jnp.repeat(heights, extent[axis_at] // shards_of).reshape([-1 if axis == axis_at else 1 for axis in range(len(extent))])
    return loudness


def setup_inputs(seed: int = 0, part: int = 0) -> dict:
    keys = jax.random.split(jax.random.key(seed), 6)
    part_keys = jax.random.split(jax.random.fold_in(keys[5], part), 6)
    section_pixels = draw_section_pixels(jax.random.fold_in(jax.random.fold_in(keys[5], part), 71), part)
    jitter_index = draw_jitter_index(jax.random.fold_in(jax.random.fold_in(keys[5], part), 71), part)
    drift_list = draw_drift_list(jax.random.fold_in(jax.random.fold_in(keys[5], part), 71), part)
    blend_weight = jnp.clip(jnp.exp(math.log(2.0) - 1.3862944 * jax.random.uniform(part_keys[3], (SECTIONS, OWNERS, OV), jnp.float32) ** block_levels(part_keys[3], (SECTIONS, OWNERS, OV), ((0, 4),), -0.2, 0.2)), 0.5, 2.0)
    patch_col = with_ends(jax.random.randint(part_keys[4], (OWNERS, N_SEC), 0, W // N_SEC - PATCH + 1), jax.random.fold_in(part_keys[4], 1), 0, (W // N_SEC - PATCH + 1) - 1).astype(jnp.int32)
    return {"section_pixels": section_pixels, "jitter_index": jitter_index, "drift_list": drift_list, "blend_weight": blend_weight, "patch_col": patch_col}


def dft_tables(length):
    indices = jnp.arange(length, dtype=jnp.int32)
    products = indices[:, None] * indices[None, :] % length
    angles = products.astype(jnp.float32) * (2.0 * math.pi / length)
    return (jnp.cos(angles), jnp.sin(angles))

def align_rows(pixels, delays):
    row_width = pixels.shape[1]
    padded = jnp.pad(pixels, ((0, 0), (0, JMAX)))
    aligned = jnp.zeros_like(pixels)
    for shift_by in range(JMAX):
        aligned = aligned + jnp.where(delays[:, None] == shift_by, padded[:, shift_by:shift_by + row_width], 0.0)
    return aligned

def row_spectra(rows):
    row_count, row_width = rows.shape
    cosine_table, sine_table = dft_tables(SEG)
    dft_table = jnp.concatenate([cosine_table, -sine_table], 1)
    spectra = jnp.dot(rows.reshape(row_count * (row_width // SEG), SEG), dft_table, precision=lax.Precision.HIGHEST, preferred_element_type=jnp.float32)
    spectra = spectra.reshape(row_count, row_width // SEG, 2 * SEG)
    return (spectra[..., :SEG], spectra[..., SEG:])

def jitter_estimate(now_real, now_imag, before_real, before_imag):
    indices = jnp.arange(SEG, dtype=jnp.int32)
    weights = jnp.sin(indices.astype(jnp.float32) * (2.0 * math.pi / SEG))
    cross_term = now_imag * before_real - now_real * before_imag
    numerator = lax.optimization_barrier(jnp.mean(weights * cross_term, axis=(1, 2)))
    power_sum = 0.5 * (now_real * now_real + now_imag * now_imag + before_real * before_real + before_imag * before_imag)
    return numerator / (lax.optimization_barrier(jnp.mean(power_sum, axis=(1, 2))) + 1e-05)

def correct_rows(aligned, jitter):
    padded = jnp.pad(aligned, ((0, 0), (1, 1)))
    slopes = 0.5 * (padded[:, 2:] - padded[:, :-2])
    return (aligned - jitter[:, None] * slopes).astype(jnp.bfloat16)

def left_mul(matrix, batch):
    return jnp.einsum('ij,...jk->...ik', matrix, batch, precision=lax.Precision.HIGHEST)

def right_mul(batch, matrix):
    return jnp.einsum('...ij,jk->...ik', batch, matrix, precision=lax.Precision.HIGHEST)

def correlate(patches):
    side = patches.shape[-1]
    cosine_table, sine_table = dft_tables(side)
    values = patches.astype(jnp.float32)
    first_cos = right_mul(values, cosine_table)
    first_sin = right_mul(values, sine_table)
    freq_real = left_mul(cosine_table, first_cos) - left_mul(sine_table, first_sin)
    freq_imag = -(left_mul(sine_table, first_cos) + left_mul(cosine_table, first_sin))
    cross_real = freq_real[:-1] * freq_real[1:] + freq_imag[:-1] * freq_imag[1:]
    cross_imag = freq_imag[:-1] * freq_real[1:] - freq_real[:-1] * freq_imag[1:]
    magnitude = jnp.sqrt(cross_real * cross_real + cross_imag * cross_imag)
    damping = 0.5 * lax.optimization_barrier(jnp.mean(magnitude, axis=(-2, -1), keepdims=True)) + 1e-06
    scaled = 1.0 / (magnitude + damping)
    damped_real = cross_real * scaled
    damped_imag = cross_imag * scaled
    back_real = right_mul(damped_real, cosine_table) - right_mul(damped_imag, sine_table)
    back_imag = right_mul(damped_real, sine_table) + right_mul(damped_imag, cosine_table)
    return (left_mul(cosine_table, back_real) - left_mul(sine_table, back_imag)) / side

def prepare(inputs):
    pixels, delays = inputs
    aligned = align_rows(pixels, delays)
    now_real, now_imag = row_spectra(aligned)
    zero_row = jnp.zeros_like(now_real[:1])
    before_real = jnp.concatenate([zero_row, now_real[:-1]], 0)
    before_imag = jnp.concatenate([zero_row, now_imag[:-1]], 0)
    jitter = jitter_estimate(now_real, now_imag, before_real, before_imag)
    return (correct_rows(aligned, jitter), jitter)

def blend_section(inputs):
    corrected, drifts, weights = inputs
    band_rows = ROWS_DEV // BLOCK
    across = W // BLOCK
    blocks = corrected.reshape(OWNERS, band_rows, BLOCK, across, BLOCK).transpose(0, 1, 3, 2, 4)
    blocks = blocks.reshape(OWNERS * NBLK, BLOCK, BLOCK).astype(jnp.float32)
    source_index = (jnp.arange(OWNERS, dtype=jnp.int32)[:, None] * NBLK + drifts[:, :, 0]).reshape(-1)
    target_index = (drifts[:, :, 1] * NBLK + drifts[:, :, 2]).reshape(-1)
    mixing = (jnp.arange(OWNERS * NBLK, dtype=jnp.int32)[:, None] == target_index[None, :]).astype(jnp.float32)
    mixing = mixing * weights.reshape(-1)[None, :]
    incoming = jnp.einsum('nm,mxy->nxy', mixing, blocks[source_index], precision=lax.Precision.HIGHEST)
    merged = (blocks + incoming) / (1.0 + lax.optimization_barrier(jnp.sum(mixing, axis=1)))[:, None, None]
    merged = merged.reshape(OWNERS, band_rows, across, BLOCK, BLOCK).transpose(0, 1, 3, 2, 4)
    return merged.reshape(ROWS, W).astype(jnp.bfloat16)

def reference(section_pixels, jitter_index, drift_list, blend_weight, patch_col):
    corrected, jitter = lax.map(prepare, (section_pixels, jitter_index))
    montage = lax.map(blend_section, (corrected, drift_list, blend_weight))
    slab_width = W // N_SEC
    patch_rows = ROWS_DEV // PATCH
    bands = montage.reshape(SECTIONS, ROWS // PATCH, PATCH, W)

    def slab_surfaces(slab_index):
        starts = slab_index * slab_width + jnp.repeat(patch_col[:, slab_index], patch_rows)
        picked = jax.vmap(lambda one_band, start_col: lax.dynamic_slice_in_dim(one_band, start_col, PATCH, 2), in_axes=(1, 0), out_axes=1)(bands, starts)
        return correlate(picked)
    surfaces = lax.map(slab_surfaces, jnp.arange(N_SEC, dtype=jnp.int32))
    return (jitter, jnp.transpose(surfaces, (1, 2, 0, 3, 4)))
```

```python
import functools
import math

import jax
import jax.numpy as jnp
import numpy as np
from jax import lax
from jax.experimental import pallas as pl
from jax.experimental.pallas import tpu as pltpu
from jax.sharding import PartitionSpec as P

SEG = 512
PATCH = 128
BLOCK = 128
CAP = 2
SUB = 8
BANDS = ("tile", "row")


def is_pow2(n):
    return n & (n - 1) == 0


def target(me, k, n):
    return me ^ k if is_pow2(n) else (me + k) % n


def origin(me, k, n):
    return me ^ k if is_pow2(n) else (me + n - k) % n


def send(x, axis, k, n):
    return lax.ppermute(x, axis, [(i, target(i, k, n)) for i in range(n)])


def has_tail(k, n):
    return any(target(i, k, n) == (i + 1) % n for i in range(n))


def find_slots(drift, band, owner, count):
    place = [jnp.int32(0)] * CAP
    found = jnp.int32(0)
    for p in range(count):
        hit = drift[0, band, p, 1] == owner
        for c in range(CAP):
            place[c] = jnp.where(hit & (found == c), p, place[c])
        found = found + jnp.where(hit, 1, 0)
    return place, found


def window_place(pcol, q, slab):
    start = q * slab + pcol[0, q]
    return start >> 7, start & (BLOCK - 1)


def split(x):
    high = x.astype(jnp.bfloat16)
    return high, (x - high.astype(jnp.float32)).astype(jnp.bfloat16)


def front_kernel(owners, secs, chunks, delay, drift, pcol, pixels, *refs):
    jitter_out, strips, first_out = refs[:3]
    messages = refs[3 : 3 + owners]
    raw, shifted, slope, wide, sums, loaded = refs[3 + owners :]
    rows, width = pixels.shape
    blocks = width // BLOCK
    per = rows // chunks
    band = lax.axis_index(BANDS)
    sec = lax.axis_index("sec")

    def load(i):
        at = pl.ds(i * per, per)
        return pltpu.make_async_copy(pixels.at[at, :], raw.at[at, :], loaded.at[i])

    for i in range(chunks):
        load(i).start()
    wide[...] = jnp.broadcast_to(delay[...], (rows, rows)).T
    shifted[:, 0:SUB, :] = jnp.zeros((blocks, SUB, BLOCK), jnp.float32)
    lane = lax.broadcasted_iota(jnp.int32, (SUB, BLOCK), 1)
    sub = lax.broadcasted_iota(jnp.int32, (SUB, BLOCK), 0)
    first_lane = lane == 0
    last_lane = lane == BLOCK - 1
    first_sub = sub == 0
    seg = SEG // BLOCK

    def eight_rows(g, _):
        at = pl.multiple_of(g * SUB, SUB)
        delays = wide[pl.ds(at, SUB), :]
        moved = lane + delays
        index = moved & (BLOCK - 1)
        near = moved < BLOCK
        picked = [
            jnp.take_along_axis(
                raw[pl.ds(at, SUB), v * BLOCK : (v + 1) * BLOCK],
                index,
                axis=1,
                mode="promise_in_bounds",
            )
            for v in range(blocks)
        ]
        picked.append(jnp.zeros((SUB, BLOCK), jnp.float32))
        x = [jnp.where(near, picked[v], picked[v + 1]) for v in range(blocks)]
        ahead = [pltpu.roll(t, BLOCK - 1, 1) for t in x]
        behind = [pltpu.roll(t, 1, 1) for t in x]
        zero = jnp.zeros((SUB, BLOCK), jnp.float32)
        cross = zero
        power = zero
        for v in range(blocks):
            nxt = ahead[v + 1] if v + 1 < blocks else zero
            prv = behind[v - 1] if v > 0 else zero
            up = jnp.where(last_lane, nxt, ahead[v])
            down = jnp.where(first_lane, prv, behind[v])
            line = up - down
            ring = line
            if v % seg == seg - 1:
                ring = jnp.where(last_lane, ahead[v + 1 - seg], ahead[v]) - down
            if v % seg == 0:
                ring = up - jnp.where(first_lane, behind[v - 1 + seg], behind[v])
            before = jnp.where(
                first_sub, shifted[v, pl.ds(at + SUB - 1, 1), :], pltpu.roll(x[v], 1, 0)
            )
            cross = cross + before * ring
            power = power + x[v] * x[v]
            shifted[v, pl.ds(at + SUB, SUB), :] = x[v]
            slope[v, pl.ds(at, SUB), :] = line
        sums[0, pl.ds(at + SUB, SUB), :] = cross
        sums[1, pl.ds(at + SUB, SUB), :] = power
        return 0

    steps = per // SUB
    for i in range(chunks):
        load(i).wait()
        lax.fori_loop(i * steps, (i + 1) * steps, eight_rows, 0)

    total_cross = jnp.sum(sums[0, SUB:, :], axis=1, keepdims=True)
    total_power = jnp.sum(sums[1, SUB:, :], axis=1, keepdims=True)
    row_index = lax.broadcasted_iota(jnp.int32, (rows, 1), 0)
    above_power = jnp.where(row_index == 0, 0.0, pltpu.roll(
        jnp.broadcast_to(total_power, (rows, BLOCK)), 1, 0))
    numerator = -jnp.where(row_index == 0, 0.0, total_cross)
    jitter = numerator / (total_power + above_power + 1e-5 * 2 * (blocks // seg))
    wide_jitter = jnp.broadcast_to(jitter, (rows, BLOCK))
    half = 0.5 * wide_jitter
    jitter_out[...] = wide_jitter.T[0:1, :]

    def corrected(n):
        return (shifted[n, SUB:, :] - half * slope[n]).astype(jnp.bfloat16)

    for v in range(blocks):
        first_out[v : v + 1, :] = shifted[v, SUB : SUB + 1, :]
        sums[0, v : v + 1, :] = shifted[v, SUB + rows - 1 : SUB + rows, :]
    first = first_out[...].astype(jnp.bfloat16)
    last, rest = split(sums[0, :blocks, :])
    count = drift.shape[2]
    for k in range(owners):
        place, _ = find_slots(drift, band, target(band, k, owners), count)
        for c in range(CAP):
            messages[k][c * BLOCK : (c + 1) * BLOCK, :] = corrected(drift[0, band, place[c], 0])
        base = CAP * BLOCK
        messages[k][base : base + blocks, :] = first
        messages[k][base + blocks : base + 2 * blocks, :] = last
        if messages[k].shape[0] > base + 2 * blocks:
            messages[k][base + 2 * blocks : base + 3 * blocks, :] = rest
    slab = width // secs
    for k in range(secs):
        n, _ = window_place(pcol, target(sec, k, secs), slab)
        strips[k, 0] = corrected(n)
        strips[k, 1] = corrected(jnp.minimum(n + 1, blocks - 1))


def row_differences(x, segmented):
    blocks = x.shape[0]
    seg = SEG // BLOCK
    lane = lax.broadcasted_iota(jnp.int32, x.shape, 1)
    block = lax.broadcasted_iota(jnp.int32, x.shape, 0)
    ahead = pltpu.roll(x, BLOCK - 1, 1)
    behind = pltpu.roll(x, 1, 1)
    last_lane = lane == BLOCK - 1
    first_lane = lane == 0
    nxt = pltpu.roll(ahead, blocks - 1, 0)
    prv = pltpu.roll(behind, 1, 0)
    line = jnp.where(last_lane, jnp.where(block == blocks - 1, 0.0, nxt), ahead) - jnp.where(
        first_lane, jnp.where(block == 0, 0.0, prv), behind
    )
    if not segmented:
        return line, None
    nxt = jnp.where(block % seg == seg - 1, pltpu.roll(ahead, seg - 1, 0), nxt)
    prv = jnp.where(block % seg == 0, pltpu.roll(behind, blocks - seg + 1, 0), prv)
    ring = jnp.where(last_lane, nxt, ahead) - jnp.where(first_lane, prv, behind)
    return line, ring


def total(x):
    return jnp.sum(jnp.sum(x, axis=1, keepdims=True), axis=0, keepdims=True)


def blend_kernel(owners, secs, drift, weight, pcol, jitter_in, strips, first, *refs):
    messages = refs[:owners]
    jitter_out = refs[owners]
    windows = refs[owners + 1 : owners + 1 + secs]
    firsts, lasts, tails, fixed, acc, den = refs[owners + 1 + secs :]
    blocks = first.shape[0]
    width = blocks * BLOCK
    seg = SEG // BLOCK
    band = lax.axis_index(BANDS)
    sec = lax.axis_index("sec")
    slab = width // secs
    slab_blocks = slab // BLOCK
    base = CAP * BLOCK
    count = drift.shape[2]
    f32 = jnp.float32
    tiny = 1e-5 * 2 * (blocks // seg)
    for k in range(owners):
        source = origin(band, k, owners)
        firsts[source] = messages[k][base : base + blocks, :].astype(f32)
        lasts[source] = messages[k][base + blocks : base + 2 * blocks, :].astype(f32)
        if messages[k].shape[0] > base + 2 * blocks:
            tails[source] = messages[k][base + 2 * blocks : base + 3 * blocks, :].astype(f32)

    def estimate(row, ring, above):
        return -total(above * ring) / (total(row * row + above * above) + tiny)

    for j in range(owners):
        row = firsts[j]
        line, ring = row_differences(row, True)
        if j == 0:
            fixed[j] = row.astype(jnp.bfloat16).astype(f32)
        else:
            half = 0.5 * estimate(row, ring, lasts[j - 1])
            fixed[j] = (row - half * line).astype(jnp.bfloat16).astype(f32)

    row = first[...]
    line, ring = row_differences(row, True)
    upper = jnp.maximum(band - 1, 0)
    own = estimate(row, ring, lasts[upper] + tails[upper])
    own = jnp.where(band == 0, 0.0, own)
    lane_row = lax.broadcasted_iota(jnp.int32, jitter_in.shape, 1)
    jitter_out[...] = jnp.where(lane_row == 0, own, jitter_in[...])

    lane = lax.broadcasted_iota(jnp.int32, (BLOCK, BLOCK), 1)
    top = lax.broadcasted_iota(jnp.int32, (BLOCK, BLOCK), 0) == 0
    lane1 = lax.broadcasted_iota(jnp.int32, (1, BLOCK), 1)

    for k in range(secs):
        n, o = window_place(pcol, target(sec, k, secs), slab)
        turn = (BLOCK - o) & (BLOCK - 1)
        near = jnp.where(top, fixed[band, pl.ds(n, 1), :], strips[k, 0].astype(f32))
        n1 = jnp.minimum(n + 1, blocks - 1)
        far = jnp.where(top, fixed[band, pl.ds(n1, 1), :], strips[k, 1].astype(f32))
        acc[target(sec, k, secs)] = jnp.where(
            lane + o < BLOCK, pltpu.roll(near, turn, 1), pltpu.roll(far, turn, 1)
        )
        den[target(sec, k, secs)] = jnp.ones((1, BLOCK), f32)

    for k in range(owners):
        source = origin(band, k, owners)
        place, found = find_slots(drift, source, band, count)
        for c in range(CAP):
            goal = drift[0, source, place[c], 2]
            q = goal // slab_blocks
            n, o = window_place(pcol, q, slab)

            @pl.when((found > c) & ((goal == n) | (goal == n + 1)))
            def _():
                w = weight[0, source, place[c]]
                turn = (BLOCK - o) & (BLOCK - 1)
                picture = messages[k][c * BLOCK : (c + 1) * BLOCK, :].astype(f32)
                origin_block = drift[0, source, place[c], 0]
                picture = jnp.where(top, fixed[source, pl.ds(origin_block, 1), :], picture)
                inside = (lane1 + o < BLOCK) == (goal == n)
                factor = jnp.where(inside, w, 0.0)
                acc[q] = acc[q] + factor * pltpu.roll(picture, turn, 1)
                den[q] = den[q] + factor

    for k in range(secs):
        q = target(sec, k, secs)
        windows[k][...] = (acc[q] * (1.0 / den[q])).astype(jnp.bfloat16)


def dot(a, b):
    return lax.dot_general(
        a,
        b,
        (((1,), (0,)), ((), ())),
        precision=lax.Precision.HIGHEST,
        preferred_element_type=jnp.float32,
    )


def surface_kernel(secs, tables, *refs):
    arrived = refs[:secs]
    out = refs[secs]
    stack = refs[secs + 1]
    sec = lax.axis_index("sec")
    side = PATCH
    for k in range(secs):
        stack[origin(sec, k, secs)] = arrived[k][...].astype(jnp.float32)
    cosine = tables[:, :side]
    sine = tables[:, side:]
    both = tables[...]
    tall = jnp.concatenate([cosine, sine], 0)
    turn = jnp.concatenate([both, jnp.concatenate([-sine, cosine], 1)], 0)
    close = jnp.concatenate([cosine, -sine], 1) * (1.0 / side)
    last = None
    for s in range(secs):
        first = dot(stack[s], both)
        grid = dot(tall, first)
        real = grid[:side, :side] - grid[side:, side:]
        imag = -(grid[side:, :side] + grid[:side, side:])
        if s > 0:
            last_real, last_imag = last
            cross_real = last_real * real + last_imag * imag
            cross_imag = last_imag * real - last_real * imag
            magnitude = jnp.sqrt(cross_real * cross_real + cross_imag * cross_imag)
            damping = (0.5 / (side * side)) * total(magnitude) + 1e-6
            scaled = 1.0 / (magnitude + damping)
            damped = jnp.concatenate([cross_real * scaled, cross_imag * scaled], 1)
            back = dot(damped, turn)
            back = jnp.concatenate([back[:, :side], back[:, side:]], 0)
            out[s - 1] = dot(close, back)
        last = (real, imag)


def dft_tables(length):
    indices = np.arange(length)
    angles = (indices[:, None] * indices[None, :] % length) * (2.0 * math.pi / length)
    return np.concatenate([np.cos(angles), np.sin(angles)], 1).astype(np.float32)


def per_device(section_pixels, jitter_index, drift_list, blend_weight, patch_col):
    pixels = section_pixels[0]
    rows, width = pixels.shape
    blocks = width // BLOCK
    owners = lax.axis_size(BANDS)
    secs = lax.axis_size("sec")
    chunks = 4
    f32, bf16 = jnp.float32, jnp.bfloat16
    vmem = pl.BlockSpec(memory_space=pltpu.VMEM)
    smem = pl.BlockSpec(memory_space=pltpu.SMEM)
    hbm = pl.BlockSpec(memory_space=pl.ANY)
    shape = jax.ShapeDtypeStruct
    message_rows = [
        CAP * BLOCK + (3 if has_tail(k, owners) else 2) * blocks for k in range(owners)
    ]
    params = pltpu.CompilerParams(vmem_limit_bytes=40 * 1024 * 1024)
    jitter, strips, first, *messages = pl.pallas_call(
        functools.partial(front_kernel, owners, secs, chunks),
        out_shape=[
            shape((1, rows), f32),
            shape((secs, 2, BLOCK, BLOCK), bf16),
            shape((blocks, BLOCK), f32),
        ]
        + [shape((r, BLOCK), bf16) for r in message_rows],
        in_specs=[vmem, smem, smem, hbm],
        out_specs=[vmem] * (3 + owners),
        scratch_shapes=[
            pltpu.VMEM((rows, width), f32),
            pltpu.VMEM((blocks, rows + SUB, BLOCK), f32),
            pltpu.VMEM((blocks, rows, BLOCK), f32),
            pltpu.VMEM((rows, rows), jnp.int32),
            pltpu.VMEM((2, rows + SUB, BLOCK), f32),
            pltpu.SemaphoreType.DMA((chunks,)),
        ],
        compiler_params=params,
        name="front",
    )(jitter_index, drift_list, patch_col, pixels)
    messages = messages[:1] + [
        send(messages[k], BANDS, k, owners) for k in range(1, owners)
    ]
    jitter, *windows = pl.pallas_call(
        functools.partial(blend_kernel, owners, secs),
        out_shape=[shape((1, rows), f32)] + [shape((PATCH, PATCH), bf16)] * secs,
        in_specs=[smem, smem, smem] + [vmem] * (3 + owners),
        out_specs=[vmem] * (1 + secs),
        scratch_shapes=[pltpu.VMEM((owners, blocks, BLOCK), f32)] * 4
        + [pltpu.VMEM((secs, PATCH, PATCH), f32), pltpu.VMEM((secs, 1, PATCH), f32)],
        compiler_params=params,
        name="blend",
    )(drift_list, blend_weight, patch_col, jitter, strips, first, *messages)
    windows = windows[:1] + [send(windows[k], "sec", k, secs) for k in range(1, secs)]
    surfaces = pl.pallas_call(
        functools.partial(surface_kernel, secs),
        out_shape=shape((secs - 1, PATCH, PATCH), f32),
        in_specs=[vmem] * (1 + secs),
        out_specs=vmem,
        scratch_shapes=[pltpu.VMEM((secs, PATCH, PATCH), f32)],
        compiler_params=params,
        name="surface",
    )(jnp.asarray(dft_tables(PATCH)), *windows)
    return (jitter, surfaces[:, None, None])


def solution(mesh):
    in_specs = (
        P(("groups", "sec"), ("tile", "row"), None),
        P(("groups", "sec"), ("tile", "row")),
        P(("groups", "sec"), None, None, None),
        P(("groups", "sec"), None, None),
        P(("tile", "row"), "groups"),
    )
    out_specs = (
        P(("groups", "sec"), ("tile", "row")),
        P("groups", ("tile", "row"), "sec", None, None),
    )
    return jax.shard_map(
        per_device, mesh=mesh, in_specs=in_specs, out_specs=out_specs, check_vma=False
    )
```

```python
import functools
import math

import jax
import jax.numpy as jnp
import numpy as np
from jax import lax
from jax.experimental import pallas as pl
from jax.experimental.pallas import tpu as pltpu
from jax.sharding import PartitionSpec as P

SEG = 512
PATCH = 128
BLOCK = 128
CAP = 2
SUB = 8
BANDS = ("tile", "row")


def is_pow2(n):
    return n & (n - 1) == 0


def target(me, k, n):
    return me ^ k if is_pow2(n) else (me + k) % n


def origin(me, k, n):
    return me ^ k if is_pow2(n) else (me + n - k) % n


def send(x, axis, k, n):
    return lax.ppermute(x, axis, [(i, target(i, k, n)) for i in range(n)])


def has_tail(k, n):
    return any(target(i, k, n) == (i + 1) % n for i in range(n))


def find_slots(drift, band, owner, count):
    place = [jnp.int32(0)] * CAP
    found = jnp.int32(0)
    for p in range(count):
        hit = drift[1, band, p] == owner
        for c in range(CAP):
            place[c] = jnp.where(hit & (found == c), p, place[c])
        found = found + jnp.where(hit, 1, 0)
    return place, found


def window_place(pcol, q, slab):
    start = q * slab + pcol[0, q]
    return start >> 7, start & (BLOCK - 1)


def split(x):
    high = x.astype(jnp.bfloat16)
    return high, (x - high.astype(jnp.float32)).astype(jnp.bfloat16)


def front_kernel(owners, chunks, delay_at, drift_at, pixels, *refs):
    jitter_out, half_out, padded, first_out = refs[:4]
    messages = refs[4 : 3 + owners]
    raw, ring, wide, sums, delay, drift, loaded = refs[3 + owners :]
    rows, width = pixels.shape
    blocks = width // BLOCK
    per = rows // chunks
    band = lax.axis_index(BANDS)

    def load(i):
        at = pl.ds(i * per, per)
        return pltpu.make_async_copy(pixels.at[at, :], raw.at[at, :], loaded.at[i])

    small = [
        pltpu.make_async_copy(a, b, loaded.at[chunks + i])
        for i, (a, b) in enumerate(((delay_at, delay), (drift_at, drift)))
    ]
    small[0].start()
    for i in range(chunks):
        load(i).start()
    small[1].start()
    padded[0] = jnp.zeros(padded.shape[1:], jnp.float32)
    padded[blocks + 1] = jnp.zeros(padded.shape[1:], jnp.float32)
    padded[1 : blocks + 1, 0:SUB, :] = jnp.zeros((blocks, SUB, BLOCK), jnp.float32)
    ring[:, 0:SUB, :] = jnp.zeros((blocks, SUB, BLOCK), jnp.float32)
    small[0].wait()
    wide[...] = jnp.broadcast_to(delay[...], (rows, rows)).T
    lane = lax.broadcasted_iota(jnp.int32, (SUB, BLOCK), 1)
    sub = lax.broadcasted_iota(jnp.int32, (SUB, BLOCK), 0)
    last_lane = lane == BLOCK - 1
    first_sub = sub == 0
    seg = SEG // BLOCK

    def eight_rows(g, _):
        at = pl.multiple_of(g * SUB, SUB)
        delays = wide[pl.ds(at, SUB), :]
        moved = lane + delays
        index = moved & (BLOCK - 1)
        near = moved < BLOCK
        picked = [
            jnp.take_along_axis(
                raw[pl.ds(at, SUB), v * BLOCK : (v + 1) * BLOCK],
                index,
                axis=1,
                mode="promise_in_bounds",
            )
            for v in range(blocks)
        ]
        picked.append(jnp.zeros((SUB, BLOCK), jnp.float32))
        x = [jnp.where(near, picked[v], picked[v + 1]) for v in range(blocks)]
        zero = jnp.zeros((SUB, BLOCK), jnp.float32)
        cross = zero
        power = zero
        for v in range(blocks):
            prv = x[v - 1] if v % seg else x[v + seg - 1]
            behind = pltpu.roll(jnp.where(last_lane, prv, x[v]), 1, 1)
            above = jnp.where(
                first_sub, padded[v + 1, pl.ds(at + SUB - 1, 1), :], pltpu.roll(x[v], 1, 0)
            )
            above_behind = jnp.where(
                first_sub, ring[v, pl.ds(at + SUB - 1, 1), :], pltpu.roll(behind, 1, 0)
            )
            cross = cross + (above * behind - above_behind * x[v])
            power = power + x[v] * x[v]
            padded[v + 1, pl.ds(at + SUB, SUB), :] = x[v]
            ring[v, pl.ds(at + SUB, SUB), :] = behind
        sums[0, pl.ds(at, SUB), :] = cross
        sums[1, pl.ds(at, SUB), :] = power
        return 0

    steps = per // SUB
    for i in range(chunks):
        load(i).wait()
        lax.fori_loop(i * steps, (i + 1) * steps, eight_rows, 0)

    small[1].wait()
    total_cross = jnp.sum(sums[0], axis=1, keepdims=True)
    total_power = jnp.sum(sums[1], axis=1, keepdims=True)
    row_index = lax.broadcasted_iota(jnp.int32, (rows, BLOCK), 0)
    power = jnp.broadcast_to(total_power, (rows, BLOCK))
    power = power + jnp.where(row_index == 0, 0.0, pltpu.roll(power, 1, 0))
    cross = jnp.broadcast_to(total_cross, (rows, BLOCK))
    jitter = cross / (power + 1e-5 * 2 * (blocks // seg))
    half = 0.5 * jitter
    half_out[...] = half
    count = drift.shape[2]
    for k in range(1, owners):
        place, _ = find_slots(drift, band, target(band, k, owners), count)
        for c in range(CAP):
            messages[k - 1][c * BLOCK : (c + 1) * BLOCK, :] = corrected(
                padded, half, drift[0, band, place[c]]
            ).astype(jnp.bfloat16)
    jitter_out[...] = jitter.T[0:1, :]
    for v in range(blocks):
        first_out[0, v : v + 1, :] = padded[v + 1, SUB : SUB + 1, :]
        first_out[1, v : v + 1, :] = padded[v + 1, SUB + rows - 1 : SUB + rows, :]
    first = first_out[0].astype(jnp.bfloat16)
    last, rest = split(first_out[1])
    base = CAP * BLOCK
    for k in range(1, owners):
        message = messages[k - 1]
        message[base : base + blocks, :] = first
        message[base + blocks : base + 2 * blocks, :] = last
        if message.shape[0] > base + 2 * blocks:
            message[base + 2 * blocks : base + 3 * blocks, :] = rest


def corrected(padded, half, n):
    rows = half.shape[0]
    here = padded[n + 1, SUB : SUB + rows, :]
    lane = lax.broadcasted_iota(jnp.int32, here.shape, 1)
    left = jnp.where(lane == BLOCK - 1, padded[n, SUB : SUB + rows, :], here)
    right = jnp.where(lane == 0, padded[n + 2, SUB : SUB + rows, :], here)
    return here - half * (pltpu.roll(right, BLOCK - 1, 1) - pltpu.roll(left, 1, 1))


def plan_kernel(owners, secs, drift, pcol, half_in, padded, acc, own):
    blocks = padded.shape[0] - 2
    slab = blocks * BLOCK // secs
    band = lax.axis_index(BANDS)
    half = half_in[...]
    lane = lax.broadcasted_iota(jnp.int32, half.shape, 1)
    place, _ = find_slots(drift, band, band, drift.shape[2])
    for c in range(CAP):
        own[c * BLOCK : (c + 1) * BLOCK, :] = corrected(
            padded, half, drift[0, band, place[c]]
        ).astype(jnp.bfloat16)
    for q in range(secs):
        n, o = window_place(pcol, q, slab)
        n1 = jnp.minimum(n + 1, blocks - 1)
        near, far = (
            corrected(padded, half, i).astype(jnp.bfloat16).astype(jnp.float32) for i in (n, n1)
        )
        picked = jnp.where(lane >= o, near, far)
        acc[q] = pltpu.roll(picked, (BLOCK - o) & (BLOCK - 1), 1)


def row_differences(x):
    blocks = x.shape[0]
    seg = SEG // BLOCK
    lane = lax.broadcasted_iota(jnp.int32, x.shape, 1)
    block = lax.broadcasted_iota(jnp.int32, x.shape, 0)
    ahead = pltpu.roll(x, BLOCK - 1, 1)
    behind = pltpu.roll(x, 1, 1)
    last_lane = lane == BLOCK - 1
    first_lane = lane == 0
    nxt = pltpu.roll(ahead, blocks - 1, 0)
    prv = pltpu.roll(behind, 1, 0)
    line = jnp.where(last_lane, jnp.where(block == blocks - 1, 0.0, nxt), ahead) - jnp.where(
        first_lane, jnp.where(block == 0, 0.0, prv), behind
    )
    nxt = jnp.where(block % seg == seg - 1, pltpu.roll(ahead, seg - 1, 0), nxt)
    prv = jnp.where(block % seg == 0, pltpu.roll(behind, blocks - seg + 1, 0), prv)
    ring = jnp.where(last_lane, nxt, ahead) - jnp.where(first_lane, prv, behind)
    return line, ring


def total(x):
    return jnp.sum(jnp.sum(x, axis=1, keepdims=True), axis=0, keepdims=True)


def blend_kernel(owners, secs, drift, weight, pcol, jitter_in, edges, begun, *refs):
    messages = refs[:owners]
    jitter_out = refs[owners]
    windows = refs[owners + 1 : owners + 1 + secs]
    firsts, lasts, tails, fixed, acc, den = refs[owners + 1 + secs :]
    blocks = edges.shape[1]
    width = blocks * BLOCK
    seg = SEG // BLOCK
    band = lax.axis_index(BANDS)
    sec = lax.axis_index("sec")
    slab = width // secs
    slab_blocks = slab // BLOCK
    base = CAP * BLOCK
    count = drift.shape[2]
    f32 = jnp.float32
    tiny = 1e-5 * 2 * (blocks // seg)
    firsts[band] = edges[0]
    lasts[band] = edges[1]
    for k in range(1, owners):
        source = origin(band, k, owners)
        firsts[source] = messages[k][base : base + blocks, :].astype(f32)
        lasts[source] = messages[k][base + blocks : base + 2 * blocks, :].astype(f32)
        if messages[k].shape[0] > base + 2 * blocks:
            tails[source] = messages[k][base + 2 * blocks : base + 3 * blocks, :].astype(f32)

    def estimate(row, ring, above):
        return -total(above * ring) / (total(row * row + above * above) + tiny)

    own = jnp.zeros((1, 1), f32)
    for j in range(owners):
        row = firsts[j]
        line, ring = row_differences(row)
        if j == 0:
            fixed[j] = row.astype(jnp.bfloat16).astype(f32)
        else:
            above = lasts[j - 1] + jnp.where(band == j, tails[j - 1], 0.0)
            found = estimate(row, ring, above)
            own = jnp.where(band == j, found, own)
            fixed[j] = (row - 0.5 * found * line).astype(jnp.bfloat16).astype(f32)
    lane_row = lax.broadcasted_iota(jnp.int32, jitter_in.shape, 1)
    jitter_out[...] = jnp.where(lane_row == 0, own, jitter_in[...])

    top = lax.broadcasted_iota(jnp.int32, (BLOCK, BLOCK), 0) == 0
    lane1 = lax.broadcasted_iota(jnp.int32, (1, BLOCK), 1)
    acc[...] = begun[...]
    for q in range(secs):
        n, o = window_place(pcol, q, slab)
        n1 = jnp.minimum(n + 1, blocks - 1)
        picked = jnp.where(lane1 >= o, fixed[band, pl.ds(n, 1), :], fixed[band, pl.ds(n1, 1), :])
        picked = pltpu.roll(jnp.broadcast_to(picked, (SUB, BLOCK)), (BLOCK - o) & (BLOCK - 1), 1)
        acc[q, 0:1, :] = picked[0:1, :]
        den[q] = jnp.ones((1, BLOCK), f32)

    for k in range(owners):
        source = origin(band, k, owners)
        place, found = find_slots(drift, source, band, count)
        for c in range(CAP):
            goal = drift[2, source, place[c]]
            q = goal // slab_blocks
            n, o = window_place(pcol, q, slab)

            @pl.when((found > c) & ((goal == n) | (goal == n + 1)))
            def _():
                w = weight[0, source, place[c]]
                turn = (BLOCK - o) & (BLOCK - 1)
                picture = messages[k][c * BLOCK : (c + 1) * BLOCK, :].astype(f32)
                origin_block = drift[0, source, place[c]]
                picture = jnp.where(top, fixed[source, pl.ds(origin_block, 1), :], picture)
                inside = (lane1 + o < BLOCK) == (goal == n)
                factor = jnp.where(inside, w, 0.0)
                acc[q] = acc[q] + factor * pltpu.roll(picture, turn, 1)
                den[q] = den[q] + factor

    for k in range(secs):
        q = target(sec, k, secs)
        windows[k][...] = (acc[q] * (1.0 / den[q])).astype(jnp.bfloat16)


def dot(a, b):
    return jnp.dot(a, b, preferred_element_type=jnp.float32)


def spectra(patches, left, right):
    side = PATCH
    found = []
    for at in range(0, len(patches), 2):
        pair = patches[at : at + 2]
        beside = jnp.concatenate(pair, 1) if len(pair) > 1 else pair[0]
        columns = dot(left, jnp.concatenate([beside, beside], 0))
        stack = []
        for i in range(len(pair)):
            high, low = split(columns[:, i * side : (i + 1) * side])
            stack.append(jnp.concatenate([high, low, high], 1))
        grid = dot(jnp.concatenate(stack, 0), right)
        for i in range(len(pair)):
            one = grid[2 * side * i : 2 * side * (i + 1)]
            real = one[:side, :side] - one[side:, side:]
            imag = -(one[side:, :side] + one[:side, side:])
            found.append((real, imag))
    return found


def spectrum_kernel(left, right, *refs):
    patches, out = refs[:-1], refs[-1]
    for k, (real, imag) in enumerate(spectra([p[...] for p in patches], left[...], right[...])):
        out[k, 0] = real
        out[k, 1] = imag


def surface_kernel(secs, left, right, turn, close, early, *refs):
    late = refs[: secs - early.shape[0]]
    out, freq, held, sent = refs[len(late) :]
    sec = lax.axis_index("sec")
    side = PATCH
    begun = early.shape[0]
    for k in range(begun):
        freq[origin(sec, k, secs)] = early[k]
    for k, (real, imag) in enumerate(spectra([p[...] for p in late], left[...], right[...])):
        at = origin(sec, begun + k, secs)
        freq[at, 0] = real
        freq[at, 1] = imag
    rows = []
    for s in range(secs - 1):
        real, imag = freq[s, 0], freq[s, 1]
        next_real, next_imag = freq[s + 1, 0], freq[s + 1, 1]
        cross_real = real * next_real + imag * next_imag
        cross_imag = imag * next_real - real * next_imag
        magnitude = jnp.sqrt(cross_real * cross_real + cross_imag * cross_imag)
        damping = (0.5 / (side * side)) * total(magnitude) + 1e-6
        scaled = 1.0 / (magnitude + damping)
        high, low = split(jnp.concatenate([cross_real * scaled, cross_imag * scaled], 1))
        rows.append(jnp.concatenate([high, low, high], 1))
    back = dot(jnp.concatenate(rows, 0), turn[...])
    copies = []
    for s in range(secs - 1):
        one = back[s * side : (s + 1) * side]
        high, low = split(jnp.concatenate([one[:, :side], one[:, side:]], 0))
        held[s] = dot(close[...], jnp.concatenate([high, low, high], 0))
        copies.append(pltpu.make_async_copy(held.at[s], out.at[s], sent.at[s]))
        copies[-1].start()
    for copy in copies:
        copy.wait()


def in_hbm(x):
    return pltpu.with_memory_space_constraint(x, pltpu.HBM)


def halves(x):
    high = x.astype(jnp.bfloat16)
    return high, (x - high.astype(np.float32)).astype(jnp.bfloat16)


def dft_tables(length):
    indices = np.arange(length)
    angles = (indices[:, None] * indices[None, :] % length) * (2.0 * math.pi / length)
    cosine, sine = np.cos(angles).astype(np.float32), np.sin(angles).astype(np.float32)
    left = np.concatenate(halves(np.concatenate([cosine, sine], 0)), 1)
    high, low = halves(np.concatenate([cosine, sine], 1))
    right = np.concatenate([high, high, low], 0)
    high, low = halves(
        np.concatenate(
            [np.concatenate([cosine, sine], 1), np.concatenate([-sine, cosine], 1)], 0
        )
    )
    turn = np.concatenate([high, high, low], 0)
    high, low = halves(np.concatenate([cosine, -sine], 1) / np.float32(length))
    close = np.concatenate([high, high, low], 1)
    return [jnp.asarray(t) for t in (left, right, turn, close)]


def per_device(section_pixels, jitter_index, drift_list, blend_weight, patch_col):
    pixels = section_pixels[0]
    rows, width = pixels.shape
    blocks = width // BLOCK
    owners = lax.axis_size(BANDS)
    secs = lax.axis_size("sec")
    chunks = 8
    drifts = jnp.transpose(drift_list[0], (2, 0, 1))
    f32, bf16 = jnp.float32, jnp.bfloat16
    vmem = pl.BlockSpec(memory_space=pltpu.VMEM)
    smem = pl.BlockSpec(memory_space=pltpu.SMEM)
    hbm = pl.BlockSpec(memory_space=pltpu.HBM)
    shape = jax.ShapeDtypeStruct
    message_rows = [
        CAP * BLOCK + (3 if has_tail(k, owners) else 2) * blocks for k in range(1, owners)
    ]
    params = pltpu.CompilerParams(vmem_limit_bytes=24 * 1024 * 1024)
    jitter, half, padded, edges, *messages = pl.pallas_call(
        functools.partial(front_kernel, owners, chunks),
        out_shape=[
            shape((1, rows), f32),
            shape((rows, BLOCK), f32),
            shape((blocks + 2, rows + SUB, BLOCK), f32),
            shape((2, blocks, BLOCK), f32),
        ]
        + [shape((r, BLOCK), bf16) for r in message_rows],
        in_specs=[hbm] * 3,
        out_specs=[vmem] * (3 + owners),
        scratch_shapes=[
            pltpu.VMEM((rows, width), f32),
            pltpu.VMEM((blocks, rows + SUB, BLOCK), f32),
            pltpu.VMEM((rows, rows), jnp.int32),
            pltpu.VMEM((2, rows, BLOCK), f32),
            pltpu.VMEM((1, rows), jnp.int32),
            pltpu.SMEM(drifts.shape, jnp.int32),
            pltpu.SemaphoreType.DMA((chunks + 2,)),
        ],
        compiler_params=params,
        name="front",
    )(*map(in_hbm, (jitter_index, drifts, pixels)))
    begun, own = pl.pallas_call(
        functools.partial(plan_kernel, owners, secs),
        out_shape=[shape((secs, PATCH, PATCH), f32), shape((CAP * BLOCK, BLOCK), bf16)],
        in_specs=[smem, smem, vmem, vmem],
        out_specs=[vmem] * 2,
        compiler_params=params,
        cost_estimate=pl.CostEstimate(flops=10**8, bytes_accessed=10**6, transcendentals=0),
        name="plan",
    )(drifts, patch_col, half, padded)
    messages = [own] + [send(messages[k - 1], BANDS, k, owners) for k in range(1, owners)]
    jitter, *windows = pl.pallas_call(
        functools.partial(blend_kernel, owners, secs),
        out_shape=[shape((1, rows), f32)] + [shape((PATCH, PATCH), bf16)] * secs,
        in_specs=[smem, smem, smem] + [vmem] * (3 + owners),
        out_specs=[vmem] * (1 + secs),
        scratch_shapes=[pltpu.VMEM((owners, blocks, BLOCK), f32)] * 4
        + [pltpu.VMEM((secs, PATCH, PATCH), f32), pltpu.VMEM((secs, 1, PATCH), f32)],
        compiler_params=params,
        name="blend",
    )(drifts, blend_weight, patch_col, jitter, edges, begun, *messages)
    windows = windows[:1] + [send(windows[k], "sec", k, secs) for k in range(1, secs)]
    left, right, turn, close = dft_tables(PATCH)
    begin = secs // 2
    early = pl.pallas_call(
        spectrum_kernel,
        out_shape=shape((begin, 2, PATCH, PATCH), f32),
        in_specs=[vmem] * (2 + begin),
        out_specs=vmem,
        compiler_params=params,
        cost_estimate=pl.CostEstimate(flops=10**8, bytes_accessed=10**6, transcendentals=0),
        name="spectrum",
    )(left, right, *windows[:begin])
    surfaces = pl.pallas_call(
        functools.partial(surface_kernel, secs),
        out_shape=shape((secs - 1, PATCH, PATCH), f32),
        in_specs=[vmem] * (5 + secs - begin),
        out_specs=hbm,
        scratch_shapes=[
            pltpu.VMEM((secs, 2, PATCH, PATCH), f32),
            pltpu.VMEM((secs - 1, PATCH, PATCH), f32),
            pltpu.SemaphoreType.DMA((secs - 1,)),
        ],
        compiler_params=params,
        name="surface",
    )(left, right, turn, close, early, *windows[begin:])
    return (jitter, surfaces[:, None, None])


def solution(mesh):
    in_specs = (
        P(("groups", "sec"), ("tile", "row"), None),
        P(("groups", "sec"), ("tile", "row")),
        P(("groups", "sec"), None, None, None),
        P(("groups", "sec"), None, None),
        P(("tile", "row"), "groups"),
    )
    out_specs = (
        P(("groups", "sec"), ("tile", "row")),
        P("groups", ("tile", "row"), "sec", None, None),
    )
    return jax.shard_map(
        per_device, mesh=mesh, in_specs=in_specs, out_specs=out_specs, check_vma=False
    )
```

```python
import functools
import math

import jax
import jax.numpy as jnp
import numpy as np
from jax import lax
from jax.experimental import pallas as pl
from jax.experimental.pallas import tpu as pltpu
from jax.sharding import PartitionSpec as P

SEG = 512
PATCH = 128
BLOCK = 128
CAP = 2
SUB = 8
PAD = 16
BANDS = ("tile", "row")


def is_pow2(n):
    return n & (n - 1) == 0


def target(me, k, n):
    return me ^ k if is_pow2(n) else (me + k) % n


def origin(me, k, n):
    return me ^ k if is_pow2(n) else (me + n - k) % n


def send(x, axis, k, n):
    return lax.ppermute(x, axis, [(i, target(i, k, n)) for i in range(n)])


def has_tail(k, n):
    return any(target(i, k, n) == (i + 1) % n for i in range(n))


def patch_order(n):
    half = n // 2
    return [0, half] + [k for k in range(n - 1, 0, -1) if k != half]


def find_slots(drift, band, owner, count):
    place = [jnp.int32(0)] * CAP
    found = jnp.int32(0)
    for p in range(count):
        hit = drift[1, band, p] == owner
        for c in range(CAP):
            place[c] = jnp.where(hit & (found == c), p, place[c])
        found = found + jnp.where(hit, 1, 0)
    return place, found


def window_place(pcol, q, slab):
    start = q * slab + pcol[0, q]
    return start >> 7, start & (BLOCK - 1)


def split(x):
    high = x.astype(jnp.bfloat16)
    return high, (x - high.astype(jnp.float32)).astype(jnp.bfloat16)


def front_kernel(owners, chunks, delay_at, drift_at, pixels, *refs):
    jitter_out, half_out, padded, first_out = refs[:4]
    messages = refs[4 : 3 + owners]
    raw, ring, wide, sums, delay, drift, loaded = refs[3 + owners :]
    rows, width = pixels.shape
    blocks = width // BLOCK
    per = rows // chunks
    band = lax.axis_index(BANDS)

    def load(i):
        at = pl.ds(i * per, per)
        return pltpu.make_async_copy(pixels.at[at, :], raw.at[at, :], loaded.at[i])

    small = [
        pltpu.make_async_copy(a, b, loaded.at[chunks + i])
        for i, (a, b) in enumerate(((delay_at, delay), (drift_at, drift)))
    ]
    small[0].start()
    for i in range(chunks):
        load(i).start()
    small[1].start()
    padded[0] = jnp.zeros(padded.shape[1:], jnp.float32)
    padded[blocks + 1] = jnp.zeros(padded.shape[1:], jnp.float32)
    padded[1 : blocks + 1, 0:PAD, :] = jnp.zeros((blocks, PAD, BLOCK), jnp.float32)
    ring[:, 0:PAD, :] = jnp.zeros((blocks, PAD, BLOCK), jnp.float32)
    small[0].wait()
    wide[...] = jnp.broadcast_to(delay[...], (rows, rows)).T
    lane = lax.broadcasted_iota(jnp.int32, (SUB, BLOCK), 1)
    last_lane = lane == BLOCK - 1
    seg = SEG // BLOCK

    def relate(at):
        cross = power = jnp.zeros((SUB, BLOCK), jnp.float32)
        here, over = pl.ds(at + PAD, SUB), pl.ds(at + (PAD - 1), SUB)
        for v in range(blocks):
            x, behind = padded[v + 1, here, :], ring[v, here, :]
            cross = cross + (padded[v + 1, over, :] * behind - ring[v, over, :] * x)
            power = power + x * x
        sums[0, pl.ds(at + SUB, SUB), :] = cross
        sums[1, pl.ds(at + SUB, SUB), :] = power

    def eight_rows(g, _):
        at = pl.multiple_of(g * SUB, SUB)
        delays = wide[pl.ds(at, SUB), :]
        moved = lane + delays
        index = moved & (BLOCK - 1)
        near = moved < BLOCK
        picked = [
            jnp.take_along_axis(
                raw[pl.ds(at, SUB), v * BLOCK : (v + 1) * BLOCK],
                index,
                axis=1,
                mode="promise_in_bounds",
            )
            for v in range(blocks)
        ]
        picked.append(jnp.zeros((SUB, BLOCK), jnp.float32))
        x = [jnp.where(near, picked[v], picked[v + 1]) for v in range(blocks)]
        for v in range(blocks):
            prv = x[v - 1] if v % seg else x[v + seg - 1]
            padded[v + 1, pl.ds(at + PAD, SUB), :] = x[v]
            ring[v, pl.ds(at + PAD, SUB), :] = pltpu.roll(jnp.where(last_lane, prv, x[v]), 1, 1)
        return 0

    def again(g, _):
        relate(pl.multiple_of(g * SUB, SUB))
        return 0

    steps = per // SUB
    for i in range(chunks):
        load(i).wait()
        lax.fori_loop(i * steps, (i + 1) * steps, eight_rows, 0, unroll=4)
        lax.fori_loop(i * steps, (i + 1) * steps, again, 0, unroll=4)

    small[1].wait()
    total_cross = jnp.sum(sums[0, SUB:], axis=1, keepdims=True)
    total_power = jnp.sum(sums[1, SUB:], axis=1, keepdims=True)
    row_index = lax.broadcasted_iota(jnp.int32, (rows, BLOCK), 0)
    power = jnp.broadcast_to(total_power, (rows, BLOCK))
    power = power + jnp.where(row_index == 0, 0.0, pltpu.roll(power, 1, 0))
    cross = jnp.broadcast_to(total_cross, (rows, BLOCK))
    jitter = cross / (power + 1e-5 * 2 * (blocks // seg))
    half = 0.5 * jitter
    half_out[...] = half
    count = drift.shape[2]
    for k in range(1, owners):
        place, _ = find_slots(drift, band, target(band, k, owners), count)
        for c in range(CAP):
            messages[k - 1][c * BLOCK : (c + 1) * BLOCK, :] = corrected(
                padded, half, drift[0, band, place[c]]
            ).astype(jnp.bfloat16)
    jitter_out[...] = jitter.T[0:1, :]
    for v in range(blocks):
        first_out[0, v : v + 1, :] = padded[v + 1, PAD : PAD + 1, :]
        first_out[1, v : v + 1, :] = padded[v + 1, PAD + rows - 1 : PAD + rows, :]
    first = first_out[0].astype(jnp.bfloat16)
    last, rest = split(first_out[1])
    base = CAP * BLOCK
    for k in range(1, owners):
        message = messages[k - 1]
        message[base : base + blocks, :] = first
        message[base + blocks : base + 2 * blocks, :] = last
        if message.shape[0] > base + 2 * blocks:
            message[base + 2 * blocks : base + 3 * blocks, :] = rest


def corrected(padded, half, n):
    rows = half.shape[0]
    here = padded[n + 1, PAD : PAD + rows, :]
    lane = lax.broadcasted_iota(jnp.int32, here.shape, 1)
    left = jnp.where(lane == BLOCK - 1, padded[n, PAD : PAD + rows, :], here)
    right = jnp.where(lane == 0, padded[n + 2, PAD : PAD + rows, :], here)
    return here - half * (pltpu.roll(right, BLOCK - 1, 1) - pltpu.roll(left, 1, 1))


def plan_kernel(owners, secs, drift, pcol, half_in, padded, acc, own):
    blocks = padded.shape[0] - 2
    slab = blocks * BLOCK // secs
    band = lax.axis_index(BANDS)
    half = half_in[...]
    lane = lax.broadcasted_iota(jnp.int32, half.shape, 1)
    place, _ = find_slots(drift, band, band, drift.shape[2])
    for c in range(CAP):
        own[c * BLOCK : (c + 1) * BLOCK, :] = corrected(
            padded, half, drift[0, band, place[c]]
        ).astype(jnp.bfloat16)
    for q in range(secs):
        n, o = window_place(pcol, q, slab)
        n1 = jnp.minimum(n + 1, blocks - 1)
        near, far = (
            corrected(padded, half, i).astype(jnp.bfloat16).astype(jnp.float32) for i in (n, n1)
        )
        picked = jnp.where(lane >= o, near, far)
        acc[q] = pltpu.roll(picked, (BLOCK - o) & (BLOCK - 1), 1)


def row_differences(x):
    blocks = x.shape[0]
    seg = SEG // BLOCK
    lane = lax.broadcasted_iota(jnp.int32, x.shape, 1)
    block = lax.broadcasted_iota(jnp.int32, x.shape, 0)
    ahead = pltpu.roll(x, BLOCK - 1, 1)
    behind = pltpu.roll(x, 1, 1)
    last_lane = lane == BLOCK - 1
    first_lane = lane == 0
    nxt = pltpu.roll(ahead, blocks - 1, 0)
    prv = pltpu.roll(behind, 1, 0)
    line = jnp.where(last_lane, jnp.where(block == blocks - 1, 0.0, nxt), ahead) - jnp.where(
        first_lane, jnp.where(block == 0, 0.0, prv), behind
    )
    nxt = jnp.where(block % seg == seg - 1, pltpu.roll(ahead, seg - 1, 0), nxt)
    prv = jnp.where(block % seg == 0, pltpu.roll(behind, blocks - seg + 1, 0), prv)
    ring = jnp.where(last_lane, nxt, ahead) - jnp.where(first_lane, prv, behind)
    return line, ring


def total(x):
    return jnp.sum(jnp.sum(x, axis=1, keepdims=True), axis=0, keepdims=True)


def blend_kernel(owners, secs, drift, weight, pcol, jitter_in, edges, begun, *refs):
    messages = refs[:owners]
    jitter_out = refs[owners]
    windows = refs[owners + 1 : owners + 1 + secs]
    firsts, lasts, tails, fixed, acc, den = refs[owners + 1 + secs :]
    blocks = edges.shape[1]
    width = blocks * BLOCK
    seg = SEG // BLOCK
    band = lax.axis_index(BANDS)
    sec = lax.axis_index("sec")
    slab = width // secs
    slab_blocks = slab // BLOCK
    base = CAP * BLOCK
    count = drift.shape[2]
    f32 = jnp.float32
    tiny = 1e-5 * 2 * (blocks // seg)
    firsts[band] = edges[0]
    lasts[band] = edges[1]
    for k in range(1, owners):
        source = origin(band, k, owners)
        firsts[source] = messages[k][base : base + blocks, :].astype(f32)
        lasts[source] = messages[k][base + blocks : base + 2 * blocks, :].astype(f32)
        if messages[k].shape[0] > base + 2 * blocks:
            tails[source] = messages[k][base + 2 * blocks : base + 3 * blocks, :].astype(f32)

    def estimate(row, ring, above):
        return -total(above * ring) / (total(row * row + above * above) + tiny)

    own = jnp.zeros((1, 1), f32)
    for j in range(owners):
        row = firsts[j]
        line, ring = row_differences(row)
        if j == 0:
            fixed[j] = row.astype(jnp.bfloat16).astype(f32)
        else:
            above = lasts[j - 1] + jnp.where(band == j, tails[j - 1], 0.0)
            found = estimate(row, ring, above)
            own = jnp.where(band == j, found, own)
            fixed[j] = (row - 0.5 * found * line).astype(jnp.bfloat16).astype(f32)
    lane_row = lax.broadcasted_iota(jnp.int32, jitter_in.shape, 1)
    jitter_out[...] = jnp.where(lane_row == 0, own, jitter_in[...])

    top = lax.broadcasted_iota(jnp.int32, (BLOCK, BLOCK), 0) == 0
    lane1 = lax.broadcasted_iota(jnp.int32, (1, BLOCK), 1)
    acc[...] = begun[...]
    for q in range(secs):
        n, o = window_place(pcol, q, slab)
        n1 = jnp.minimum(n + 1, blocks - 1)
        picked = jnp.where(lane1 >= o, fixed[band, pl.ds(n, 1), :], fixed[band, pl.ds(n1, 1), :])
        picked = pltpu.roll(jnp.broadcast_to(picked, (SUB, BLOCK)), (BLOCK - o) & (BLOCK - 1), 1)
        acc[q, 0:1, :] = picked[0:1, :]
        den[q] = jnp.ones((1, BLOCK), f32)

    for k in range(owners):
        source = origin(band, k, owners)
        place, found = find_slots(drift, source, band, count)
        for c in range(CAP):
            goal = drift[2, source, place[c]]
            q = goal // slab_blocks
            n, o = window_place(pcol, q, slab)

            @pl.when((found > c) & ((goal == n) | (goal == n + 1)))
            def _():
                w = weight[0, source, place[c]]
                turn = (BLOCK - o) & (BLOCK - 1)
                picture = messages[k][c * BLOCK : (c + 1) * BLOCK, :].astype(f32)
                origin_block = drift[0, source, place[c]]
                picture = jnp.where(top, fixed[source, pl.ds(origin_block, 1), :], picture)
                inside = (lane1 + o < BLOCK) == (goal == n)
                factor = jnp.where(inside, w, 0.0)
                acc[q] = acc[q] + factor * pltpu.roll(picture, turn, 1)
                den[q] = den[q] + factor

    for k in range(secs):
        q = target(sec, k, secs)
        windows[k][...] = (acc[q] * (1.0 / den[q])).astype(jnp.bfloat16)


def dot(a, b):
    return jnp.dot(a, b, preferred_element_type=jnp.float32)


def spectra(patches, left, right):
    side = PATCH
    found = []
    for at in range(0, len(patches), 2):
        pair = patches[at : at + 2]
        beside = jnp.concatenate(pair, 1) if len(pair) > 1 else pair[0]
        columns = dot(left, jnp.concatenate([beside, beside], 0))
        stack = []
        for i in range(len(pair)):
            high, low = split(columns[:, i * side : (i + 1) * side])
            stack.append(jnp.concatenate([high, low, high], 1))
        grid = dot(jnp.concatenate(stack, 0), right)
        for i in range(len(pair)):
            one = grid[2 * side * i : 2 * side * (i + 1)]
            real = one[:side, :side] - one[side:, side:]
            imag = -(one[side:, :side] + one[:side, side:])
            found.append((real, imag))
    return found


def spectrum_kernel(left, right, *refs):
    patches, out = refs[:-1], refs[-1]
    for k, (real, imag) in enumerate(spectra([p[...] for p in patches], left[...], right[...])):
        out[k, 0] = real
        out[k, 1] = imag


def surface_kernel(secs, left, right, turn, close, early, *refs):
    late = refs[: secs - early.shape[0]]
    out, freq, held, sent = refs[len(late) :]
    sec = lax.axis_index("sec")
    side = PATCH
    begun = early.shape[0]
    order = patch_order(secs)
    for k in range(begun):
        freq[origin(sec, order[k], secs)] = early[k]
    for k, (real, imag) in enumerate(spectra([p[...] for p in late], left[...], right[...])):
        at = origin(sec, order[begun + k], secs)
        freq[at, 0] = real
        freq[at, 1] = imag
    rows = []
    for s in range(secs - 1):
        real, imag = freq[s, 0], freq[s, 1]
        next_real, next_imag = freq[s + 1, 0], freq[s + 1, 1]
        cross_real = real * next_real + imag * next_imag
        cross_imag = imag * next_real - real * next_imag
        magnitude = jnp.sqrt(cross_real * cross_real + cross_imag * cross_imag)
        damping = (0.5 / (side * side)) * total(magnitude) + 1e-6
        scaled = 1.0 / (magnitude + damping)
        high, low = split(jnp.concatenate([cross_real * scaled, cross_imag * scaled], 1))
        rows.append(jnp.concatenate([high, low, high], 1))
    back = dot(jnp.concatenate(rows, 0), turn[...])
    copies = []
    for s in range(secs - 1):
        one = back[s * side : (s + 1) * side]
        high, low = split(jnp.concatenate([one[:, :side], one[:, side:]], 0))
        held[s] = dot(close[...], jnp.concatenate([high, low, high], 0))
        copies.append(pltpu.make_async_copy(held.at[s], out.at[s], sent.at[s]))
        copies[-1].start()
    for copy in copies:
        copy.wait()


def in_hbm(x):
    return pltpu.with_memory_space_constraint(x, pltpu.HBM)


def halves(x):
    high = x.astype(jnp.bfloat16)
    return high, (x - high.astype(np.float32)).astype(jnp.bfloat16)


def dft_tables(length):
    indices = np.arange(length)
    angles = (indices[:, None] * indices[None, :] % length) * (2.0 * math.pi / length)
    cosine, sine = np.cos(angles).astype(np.float32), np.sin(angles).astype(np.float32)
    left = np.concatenate(halves(np.concatenate([cosine, sine], 0)), 1)
    high, low = halves(np.concatenate([cosine, sine], 1))
    right = np.concatenate([high, high, low], 0)
    high, low = halves(
        np.concatenate(
            [np.concatenate([cosine, sine], 1), np.concatenate([-sine, cosine], 1)], 0
        )
    )
    turn = np.concatenate([high, high, low], 0)
    high, low = halves(np.concatenate([cosine, -sine], 1) / np.float32(length))
    close = np.concatenate([high, high, low], 1)
    return [jnp.asarray(t) for t in (left, right, turn, close)]


def per_device(section_pixels, jitter_index, drift_list, blend_weight, patch_col):
    pixels = section_pixels[0]
    rows, width = pixels.shape
    blocks = width // BLOCK
    owners = lax.axis_size(BANDS)
    secs = lax.axis_size("sec")
    chunks = 4
    drifts = jnp.transpose(drift_list[0], (2, 0, 1))
    f32, bf16 = jnp.float32, jnp.bfloat16
    vmem = pl.BlockSpec(memory_space=pltpu.VMEM)
    smem = pl.BlockSpec(memory_space=pltpu.SMEM)
    hbm = pl.BlockSpec(memory_space=pltpu.HBM)
    shape = jax.ShapeDtypeStruct
    message_rows = [
        CAP * BLOCK + (3 if has_tail(k, owners) else 2) * blocks for k in range(1, owners)
    ]
    params = pltpu.CompilerParams(vmem_limit_bytes=24 * 1024 * 1024)
    jitter, half, padded, edges, *messages = pl.pallas_call(
        functools.partial(front_kernel, owners, chunks),
        out_shape=[
            shape((1, rows), f32),
            shape((rows, BLOCK), f32),
            shape((blocks + 2, rows + PAD, BLOCK), f32),
            shape((2, blocks, BLOCK), f32),
        ]
        + [shape((r, BLOCK), bf16) for r in message_rows],
        in_specs=[hbm] * 3,
        out_specs=[vmem] * (3 + owners),
        scratch_shapes=[
            pltpu.VMEM((rows, width), f32),
            pltpu.VMEM((blocks, rows + PAD, BLOCK), f32),
            pltpu.VMEM((rows, rows), jnp.int32),
            pltpu.VMEM((2, rows + SUB, BLOCK), f32),
            pltpu.VMEM((1, rows), jnp.int32),
            pltpu.SMEM(drifts.shape, jnp.int32),
            pltpu.SemaphoreType.DMA((chunks + 2,)),
        ],
        compiler_params=params,
        name="front",
    )(*map(in_hbm, (jitter_index, drifts, pixels)))
    begun, own = pl.pallas_call(
        functools.partial(plan_kernel, owners, secs),
        out_shape=[shape((secs, PATCH, PATCH), f32), shape((CAP * BLOCK, BLOCK), bf16)],
        in_specs=[smem, smem, vmem, vmem],
        out_specs=[vmem] * 2,
        compiler_params=params,
        cost_estimate=pl.CostEstimate(flops=10**8, bytes_accessed=10**6, transcendentals=0),
        name="plan",
    )(drifts, patch_col, half, padded)
    messages = [own] + [send(messages[k - 1], BANDS, k, owners) for k in range(1, owners)]
    jitter, *windows = pl.pallas_call(
        functools.partial(blend_kernel, owners, secs),
        out_shape=[shape((1, rows), f32)] + [shape((PATCH, PATCH), bf16)] * secs,
        in_specs=[smem, smem, smem] + [vmem] * (3 + owners),
        out_specs=[vmem] * (1 + secs),
        scratch_shapes=[pltpu.VMEM((owners, blocks, BLOCK), f32)] * 4
        + [pltpu.VMEM((secs, PATCH, PATCH), f32), pltpu.VMEM((secs, 1, PATCH), f32)],
        compiler_params=params,
        name="blend",
    )(drifts, blend_weight, patch_col, jitter, edges, begun, *messages)
    order = patch_order(secs)
    windows = windows[:1] + [send(windows[k], "sec", k, secs) for k in order[1:]]
    left, right, turn, close = dft_tables(PATCH)
    begin = secs // 2
    early = pl.pallas_call(
        spectrum_kernel,
        out_shape=shape((begin, 2, PATCH, PATCH), f32),
        in_specs=[vmem] * (2 + begin),
        out_specs=vmem,
        compiler_params=params,
        cost_estimate=pl.CostEstimate(flops=10**8, bytes_accessed=10**6, transcendentals=0),
        name="spectrum",
    )(left, right, *windows[:begin])
    surfaces = pl.pallas_call(
        functools.partial(surface_kernel, secs),
        out_shape=shape((secs - 1, PATCH, PATCH), f32),
        in_specs=[vmem] * (5 + secs - begin),
        out_specs=hbm,
        scratch_shapes=[
            pltpu.VMEM((secs, 2, PATCH, PATCH), f32),
            pltpu.VMEM((secs - 1, PATCH, PATCH), f32),
            pltpu.SemaphoreType.DMA((secs - 1,)),
        ],
        compiler_params=params,
        name="surface",
    )(left, right, turn, close, early, *windows[begin:])
    return (jitter, surfaces[:, None, None])


def solution(mesh):
    in_specs = (
        P(("groups", "sec"), ("tile", "row"), None),
        P(("groups", "sec"), ("tile", "row")),
        P(("groups", "sec"), None, None, None),
        P(("groups", "sec"), None, None),
        P(("tile", "row"), "groups"),
    )
    out_specs = (
        P(("groups", "sec"), ("tile", "row")),
        P("groups", ("tile", "row"), "sec", None, None),
    )
    return jax.shard_map(
        per_device, mesh=mesh, in_specs=in_specs, out_specs=out_specs, check_vma=False
    )
```

```python
import functools
import math

import jax
import jax.numpy as jnp
import numpy as np
from jax import lax
from jax.experimental import pallas as pl
from jax.experimental.pallas import tpu as pltpu
from jax.sharding import PartitionSpec as P

SEG = 512
PATCH = 128
BLOCK = 128
CAP = 2
SUB = 8
NOTE = 5
PAD = 16
BANDS = ("tile", "row")


def is_pow2(n):
    return n & (n - 1) == 0


def target(me, k, n):
    return me ^ k if is_pow2(n) else (me + k) % n


def origin(me, k, n):
    return me ^ k if is_pow2(n) else (me + n - k) % n


def send(x, axis, k, n):
    return lax.ppermute(x, axis, [(i, target(i, k, n)) for i in range(n)])


def has_tail(k, n):
    return any(target(i, k, n) == (i + 1) % n for i in range(n))


def patch_order(n):
    half = n // 2
    return [0, half] + [k for k in range(n - 1, 0, -1) if k != half]


def find_slots(drift, band, owner, count):
    place = [jnp.int32(0)] * CAP
    found = jnp.int32(0)
    for p in range(count):
        hit = drift[1, band, p] == owner
        for c in range(CAP):
            place[c] = jnp.where(hit & (found == c), p, place[c])
        found = found + jnp.where(hit, 1, 0)
    return place, found


def window_place(pcol, q, slab):
    start = q * slab + pcol[0, q]
    return start >> 7, start & (BLOCK - 1)


def split(x):
    high = x.astype(jnp.bfloat16)
    return high, (x - high.astype(jnp.float32)).astype(jnp.bfloat16)


def front_kernel(owners, chunks, delay_at, drift_at, pixels, *refs):
    jitter_out, half_out, padded, first_out = refs[:4]
    messages = refs[4 : 3 + owners]
    raw, ring, wide, sums, delay, drift, loaded = refs[3 + owners :]
    rows, width = pixels.shape
    blocks = width // BLOCK
    per = rows // chunks
    band = lax.axis_index(BANDS)

    def load(i):
        at = pl.ds(i * per, per)
        return pltpu.make_async_copy(pixels.at[at, :], raw.at[at, :], loaded.at[i])

    small = [
        pltpu.make_async_copy(a, b, loaded.at[chunks + i])
        for i, (a, b) in enumerate(((delay_at, delay), (drift_at, drift)))
    ]
    small[0].start()
    for i in range(chunks):
        load(i).start()
    small[1].start()
    padded[0] = jnp.zeros(padded.shape[1:], jnp.float32)
    padded[blocks + 1] = jnp.zeros(padded.shape[1:], jnp.float32)
    padded[1 : blocks + 1, 0:PAD, :] = jnp.zeros((blocks, PAD, BLOCK), jnp.float32)
    ring[:, 0:PAD, :] = jnp.zeros((blocks, PAD, BLOCK), jnp.float32)
    small[0].wait()
    wide[...] = jnp.broadcast_to(delay[...], (rows, rows)).T
    lane = lax.broadcasted_iota(jnp.int32, (SUB, BLOCK), 1)
    last_lane = lane == BLOCK - 1
    seg = SEG // BLOCK

    def relate(at):
        cross = power = jnp.zeros((SUB, BLOCK), jnp.float32)
        here, over = pl.ds(at + PAD, SUB), pl.ds(at + (PAD - 1), SUB)
        for v in range(blocks):
            x, behind = padded[v + 1, here, :], ring[v, here, :]
            cross = cross + (padded[v + 1, over, :] * behind - ring[v, over, :] * x)
            power = power + x * x
        sums[0, pl.ds(at + SUB, SUB), :] = cross
        sums[1, pl.ds(at + SUB, SUB), :] = power

    def eight_rows(g, _):
        at = pl.multiple_of(g * SUB, SUB)
        delays = wide[pl.ds(at, SUB), :]
        moved = lane + delays
        index = moved & (BLOCK - 1)
        near = moved < BLOCK
        picked = [
            jnp.take_along_axis(
                raw[pl.ds(at, SUB), v * BLOCK : (v + 1) * BLOCK],
                index,
                axis=1,
                mode="promise_in_bounds",
            )
            for v in range(blocks)
        ]
        picked.append(jnp.zeros((SUB, BLOCK), jnp.float32))
        x = [jnp.where(near, picked[v], picked[v + 1]) for v in range(blocks)]
        for v in range(blocks):
            prv = x[v - 1] if v % seg else x[v + seg - 1]
            padded[v + 1, pl.ds(at + PAD, SUB), :] = x[v]
            ring[v, pl.ds(at + PAD, SUB), :] = pltpu.roll(jnp.where(last_lane, prv, x[v]), 1, 1)
        return 0

    def again(g, _):
        relate(pl.multiple_of(g * SUB, SUB))
        return 0

    steps = per // SUB
    for i in range(chunks):
        load(i).wait()
        lax.fori_loop(i * steps, (i + 1) * steps, eight_rows, 0, unroll=4)
        lax.fori_loop(i * steps, (i + 1) * steps, again, 0, unroll=4)

    small[1].wait()
    total_cross = jnp.sum(sums[0, SUB:], axis=1, keepdims=True)
    total_power = jnp.sum(sums[1, SUB:], axis=1, keepdims=True)
    row_index = lax.broadcasted_iota(jnp.int32, (rows, BLOCK), 0)
    power = jnp.broadcast_to(total_power, (rows, BLOCK))
    power = power + jnp.where(row_index == 0, 0.0, pltpu.roll(power, 1, 0))
    cross = jnp.broadcast_to(total_cross, (rows, BLOCK))
    jitter = cross / (power + 1e-5 * 2 * (blocks // seg))
    half = 0.5 * jitter
    half_out[...] = half
    count = drift.shape[2]
    for k in range(1, owners):
        place, _ = find_slots(drift, band, target(band, k, owners), count)
        for c in range(CAP):
            messages[k - 1][c * BLOCK : (c + 1) * BLOCK, :] = corrected(
                padded, half, drift[0, band, place[c]]
            ).astype(jnp.bfloat16)
    jitter_out[...] = jitter.T[0:1, :]
    for v in range(blocks):
        first_out[0, v : v + 1, :] = padded[v + 1, PAD : PAD + 1, :]
        first_out[1, v : v + 1, :] = padded[v + 1, PAD + rows - 1 : PAD + rows, :]
    first = first_out[0].astype(jnp.bfloat16)
    last, rest = split(first_out[1])
    base = CAP * BLOCK
    for k in range(1, owners):
        message = messages[k - 1]
        message[base : base + blocks, :] = first
        message[base + blocks : base + 2 * blocks, :] = last
        if message.shape[0] > base + 2 * blocks:
            message[base + 2 * blocks : base + 3 * blocks, :] = rest


def corrected(padded, half, n):
    rows = half.shape[0]
    here = padded[n + 1, PAD : PAD + rows, :]
    lane = lax.broadcasted_iota(jnp.int32, here.shape, 1)
    left = jnp.where(lane == BLOCK - 1, padded[n, PAD : PAD + rows, :], here)
    right = jnp.where(lane == 0, padded[n + 2, PAD : PAD + rows, :], here)
    return here - half * (pltpu.roll(right, BLOCK - 1, 1) - pltpu.roll(left, 1, 1))


def plan_kernel(owners, secs, drift, weight, pcol, half_in, padded, acc, own, notes, shares):
    blocks = padded.shape[0] - 2
    slab = blocks * BLOCK // secs
    band = lax.axis_index(BANDS)
    half = half_in[...]
    lane = lax.broadcasted_iota(jnp.int32, half.shape, 1)
    place, _ = find_slots(drift, band, band, drift.shape[2])
    for c in range(CAP):
        own[c * BLOCK : (c + 1) * BLOCK, :] = corrected(
            padded, half, drift[0, band, place[c]]
        ).astype(jnp.bfloat16)
    for q in range(secs):
        n, o = window_place(pcol, q, slab)
        n1 = jnp.minimum(n + 1, blocks - 1)
        near, far = (
            corrected(padded, half, i).astype(jnp.bfloat16).astype(jnp.float32) for i in (n, n1)
        )
        picked = jnp.where(lane >= o, near, far)
        acc[q] = pltpu.roll(picked, (BLOCK - o) & (BLOCK - 1), 1)
        notes[owners * CAP * NOTE + 2 * q] = n
        notes[owners * CAP * NOTE + 2 * q + 1] = o
    for k in range(owners):
        source = origin(band, k, owners)
        place, found = find_slots(drift, source, band, drift.shape[2])
        for c in range(CAP):
            goal = drift[2, source, place[c]]
            q = goal // (slab // BLOCK)
            n, o = window_place(pcol, q, slab)
            hit = (found > c) & ((goal == n) | (goal == n + 1))
            at = (k * CAP + c) * NOTE
            notes[at] = jnp.where(hit, 1, 0)
            notes[at + 1] = q
            notes[at + 2] = o
            notes[at + 3] = jnp.where(goal == n, 1, 0)
            notes[at + 4] = drift[0, source, place[c]]
            shares[k * CAP + c] = weight[0, source, place[c]]


def row_differences(x):
    blocks = x.shape[0]
    seg = SEG // BLOCK
    lane = lax.broadcasted_iota(jnp.int32, x.shape, 1)
    block = lax.broadcasted_iota(jnp.int32, x.shape, 0)
    ahead = pltpu.roll(x, BLOCK - 1, 1)
    behind = pltpu.roll(x, 1, 1)
    last_lane = lane == BLOCK - 1
    first_lane = lane == 0
    nxt = pltpu.roll(ahead, blocks - 1, 0)
    prv = pltpu.roll(behind, 1, 0)
    line = jnp.where(last_lane, jnp.where(block == blocks - 1, 0.0, nxt), ahead) - jnp.where(
        first_lane, jnp.where(block == 0, 0.0, prv), behind
    )
    nxt = jnp.where(block % seg == seg - 1, pltpu.roll(ahead, seg - 1, 0), nxt)
    prv = jnp.where(block % seg == 0, pltpu.roll(behind, blocks - seg + 1, 0), prv)
    ring = jnp.where(last_lane, nxt, ahead) - jnp.where(first_lane, prv, behind)
    return line, ring


def total(x):
    return jnp.sum(jnp.sum(x, axis=1, keepdims=True), axis=0, keepdims=True)


def blend_kernel(owners, secs, notes, shares, jitter_in, edges, begun, *refs):
    messages = refs[:owners]
    jitter_out = refs[owners]
    windows = refs[owners + 1 : owners + 1 + secs]
    firsts, lasts, tails, fixed, acc, den = refs[owners + 1 + secs :]
    blocks = edges.shape[1]
    seg = SEG // BLOCK
    band = lax.axis_index(BANDS)
    sec = lax.axis_index("sec")
    base = CAP * BLOCK
    f32 = jnp.float32
    tiny = 1e-5 * 2 * (blocks // seg)
    firsts[band] = edges[0]
    lasts[band] = edges[1]
    for k in range(1, owners):
        source = origin(band, k, owners)
        firsts[source] = messages[k][base : base + blocks, :].astype(f32)
        lasts[source] = messages[k][base + blocks : base + 2 * blocks, :].astype(f32)
        if messages[k].shape[0] > base + 2 * blocks:
            tails[source] = messages[k][base + 2 * blocks : base + 3 * blocks, :].astype(f32)

    def estimate(row, ring, above):
        return -total(above * ring) / (total(row * row + above * above) + tiny)

    own = jnp.zeros((1, 1), f32)
    for j in range(owners):
        row = firsts[j]
        line, ring = row_differences(row)
        if j == 0:
            fixed[j] = row.astype(jnp.bfloat16).astype(f32)
        else:
            above = lasts[j - 1] + jnp.where(band == j, tails[j - 1], 0.0)
            found = estimate(row, ring, above)
            own = jnp.where(band == j, found, own)
            fixed[j] = (row - 0.5 * found * line).astype(jnp.bfloat16).astype(f32)
    lane_row = lax.broadcasted_iota(jnp.int32, jitter_in.shape, 1)
    jitter_out[...] = jnp.where(lane_row == 0, own, jitter_in[...])

    top = lax.broadcasted_iota(jnp.int32, (BLOCK, BLOCK), 0) == 0
    lane1 = lax.broadcasted_iota(jnp.int32, (1, BLOCK), 1)
    acc[...] = begun[...]
    for q in range(secs):
        n = notes[owners * CAP * NOTE + 2 * q]
        o = notes[owners * CAP * NOTE + 2 * q + 1]
        n1 = jnp.minimum(n + 1, blocks - 1)
        picked = jnp.where(lane1 >= o, fixed[band, pl.ds(n, 1), :], fixed[band, pl.ds(n1, 1), :])
        picked = pltpu.roll(jnp.broadcast_to(picked, (SUB, BLOCK)), (BLOCK - o) & (BLOCK - 1), 1)
        acc[q, 0:1, :] = picked[0:1, :]
        den[q] = jnp.ones((1, BLOCK), f32)

    for k in range(owners):
        source = origin(band, k, owners)
        for c in range(CAP):
            at = (k * CAP + c) * NOTE

            @pl.when(notes[at] > 0)
            def _():
                q, o = notes[at + 1], notes[at + 2]
                w = shares[k * CAP + c]
                turn = (BLOCK - o) & (BLOCK - 1)
                picture = messages[k][c * BLOCK : (c + 1) * BLOCK, :].astype(f32)
                origin_block = notes[at + 4]
                picture = jnp.where(top, fixed[source, pl.ds(origin_block, 1), :], picture)
                inside = (lane1 + o < BLOCK) == (notes[at + 3] > 0)
                factor = jnp.where(inside, w, 0.0)
                acc[q] = acc[q] + factor * pltpu.roll(picture, turn, 1)
                den[q] = den[q] + factor

    for k in range(secs):
        q = target(sec, k, secs)
        windows[k][...] = (acc[q] * (1.0 / den[q])).astype(jnp.bfloat16)


def dot(a, b):
    return jnp.dot(a, b, preferred_element_type=jnp.float32)


def spectra(patches, left, right):
    side = PATCH
    found = []
    for at in range(0, len(patches), 2):
        pair = patches[at : at + 2]
        beside = jnp.concatenate(pair, 1) if len(pair) > 1 else pair[0]
        columns = dot(left, jnp.concatenate([beside, beside], 0))
        stack = []
        for i in range(len(pair)):
            high, low = split(columns[:, i * side : (i + 1) * side])
            stack.append(jnp.concatenate([high, low, high], 1))
        grid = dot(jnp.concatenate(stack, 0), right)
        for i in range(len(pair)):
            one = grid[2 * side * i : 2 * side * (i + 1)]
            real = one[:side, :side] - one[side:, side:]
            imag = -(one[side:, :side] + one[:side, side:])
            found.append((real, imag))
    return found


def spectrum_kernel(left, right, *refs):
    patches, out = refs[:-1], refs[-1]
    for k, (real, imag) in enumerate(spectra([p[...] for p in patches], left[...], right[...])):
        out[k, 0] = real
        out[k, 1] = imag


def surface_kernel(secs, left, right, turn, close, early, *refs):
    late = refs[: secs - early.shape[0]]
    out, freq, held, sent = refs[len(late) :]
    sec = lax.axis_index("sec")
    side = PATCH
    begun = early.shape[0]
    order = patch_order(secs)
    for k in range(begun):
        freq[origin(sec, order[k], secs)] = early[k]
    for k, (real, imag) in enumerate(spectra([p[...] for p in late], left[...], right[...])):
        at = origin(sec, order[begun + k], secs)
        freq[at, 0] = real
        freq[at, 1] = imag
    rows = []
    for s in range(secs - 1):
        real, imag = freq[s, 0], freq[s, 1]
        next_real, next_imag = freq[s + 1, 0], freq[s + 1, 1]
        cross_real = real * next_real + imag * next_imag
        cross_imag = imag * next_real - real * next_imag
        magnitude = jnp.sqrt(cross_real * cross_real + cross_imag * cross_imag)
        damping = (0.5 / (side * side)) * total(magnitude) + 1e-6
        scaled = 1.0 / (magnitude + damping)
        high, low = split(jnp.concatenate([cross_real * scaled, cross_imag * scaled], 1))
        rows.append(jnp.concatenate([high, low, high], 1))
    back = dot(jnp.concatenate(rows, 0), turn[...])
    copies = []
    for s in range(secs - 1):
        one = back[s * side : (s + 1) * side]
        high, low = split(jnp.concatenate([one[:, :side], one[:, side:]], 0))
        held[s] = dot(close[...], jnp.concatenate([high, low, high], 0))
        copies.append(pltpu.make_async_copy(held.at[s], out.at[s], sent.at[s]))
        copies[-1].start()
    for copy in copies:
        copy.wait()


def in_hbm(x):
    return pltpu.with_memory_space_constraint(x, pltpu.HBM)


def in_smem(x):
    return pltpu.with_memory_space_constraint(x, pltpu.SMEM)


def halves(x):
    high = x.astype(jnp.bfloat16)
    return high, (x - high.astype(np.float32)).astype(jnp.bfloat16)


def dft_tables(length):
    indices = np.arange(length)
    angles = (indices[:, None] * indices[None, :] % length) * (2.0 * math.pi / length)
    cosine, sine = np.cos(angles).astype(np.float32), np.sin(angles).astype(np.float32)
    left = np.concatenate(halves(np.concatenate([cosine, sine], 0)), 1)
    high, low = halves(np.concatenate([cosine, sine], 1))
    right = np.concatenate([high, high, low], 0)
    high, low = halves(
        np.concatenate(
            [np.concatenate([cosine, sine], 1), np.concatenate([-sine, cosine], 1)], 0
        )
    )
    turn = np.concatenate([high, high, low], 0)
    high, low = halves(np.concatenate([cosine, -sine], 1) / np.float32(length))
    close = np.concatenate([high, high, low], 1)
    return [jnp.asarray(t) for t in (left, right, turn, close)]


def per_device(section_pixels, jitter_index, drift_list, blend_weight, patch_col):
    pixels = section_pixels[0]
    rows, width = pixels.shape
    blocks = width // BLOCK
    owners = lax.axis_size(BANDS)
    secs = lax.axis_size("sec")
    chunks = 4
    drifts = jnp.transpose(drift_list[0], (2, 0, 1))
    f32, bf16 = jnp.float32, jnp.bfloat16
    vmem = pl.BlockSpec(memory_space=pltpu.VMEM)
    smem = pl.BlockSpec(memory_space=pltpu.SMEM)
    hbm = pl.BlockSpec(memory_space=pltpu.HBM)
    shape = jax.ShapeDtypeStruct
    message_rows = [
        CAP * BLOCK + (3 if has_tail(k, owners) else 2) * blocks for k in range(1, owners)
    ]
    params = pltpu.CompilerParams(vmem_limit_bytes=24 * 1024 * 1024)
    jitter, half, padded, edges, *messages = pl.pallas_call(
        functools.partial(front_kernel, owners, chunks),
        out_shape=[
            shape((1, rows), f32),
            shape((rows, BLOCK), f32),
            shape((blocks + 2, rows + PAD, BLOCK), f32),
            shape((2, blocks, BLOCK), f32),
        ]
        + [shape((r, BLOCK), bf16) for r in message_rows],
        in_specs=[hbm] * 3,
        out_specs=[vmem] * (3 + owners),
        scratch_shapes=[
            pltpu.VMEM((rows, width), f32),
            pltpu.VMEM((blocks, rows + PAD, BLOCK), f32),
            pltpu.VMEM((rows, rows), jnp.int32),
            pltpu.VMEM((2, rows + SUB, BLOCK), f32),
            pltpu.VMEM((1, rows), jnp.int32),
            pltpu.SMEM(drifts.shape, jnp.int32),
            pltpu.SemaphoreType.DMA((chunks + 2,)),
        ],
        compiler_params=params,
        name="front",
    )(*map(in_hbm, (jitter_index, drifts, pixels)))
    begun, own, notes, shares = pl.pallas_call(
        functools.partial(plan_kernel, owners, secs),
        out_shape=[
            shape((secs, PATCH, PATCH), f32),
            shape((CAP * BLOCK, BLOCK), bf16),
            pltpu.SMEM((owners * CAP * NOTE + 2 * secs,), jnp.int32),
            pltpu.SMEM((owners * CAP,), f32),
        ],
        in_specs=[smem, smem, smem, vmem, vmem],
        out_specs=[vmem, vmem, smem, smem],
        compiler_params=params,
        cost_estimate=pl.CostEstimate(flops=10**8, bytes_accessed=10**6, transcendentals=0),
        name="plan",
    )(drifts, blend_weight, patch_col, half, padded)
    messages = [own] + [send(messages[k - 1], BANDS, k, owners) for k in range(1, owners)]
    jitter, *windows = pl.pallas_call(
        functools.partial(blend_kernel, owners, secs),
        out_shape=[shape((1, rows), f32)] + [shape((PATCH, PATCH), bf16)] * secs,
        in_specs=[smem, smem] + [vmem] * (3 + owners),
        out_specs=[vmem] * (1 + secs),
        scratch_shapes=[pltpu.VMEM((owners, blocks, BLOCK), f32)] * 4
        + [pltpu.VMEM((secs, PATCH, PATCH), f32), pltpu.VMEM((secs, 1, PATCH), f32)],
        compiler_params=params,
        name="blend",
    )(in_smem(notes), in_smem(shares), jitter, edges, begun, *messages)
    order = patch_order(secs)
    windows = windows[:1] + [send(windows[k], "sec", k, secs) for k in order[1:]]
    left, right, turn, close = dft_tables(PATCH)
    begin = secs // 2
    early = pl.pallas_call(
        spectrum_kernel,
        out_shape=shape((begin, 2, PATCH, PATCH), f32),
        in_specs=[vmem] * (2 + begin),
        out_specs=vmem,
        compiler_params=params,
        cost_estimate=pl.CostEstimate(flops=10**8, bytes_accessed=10**6, transcendentals=0),
        name="spectrum",
    )(left, right, *windows[:begin])
    surfaces = pl.pallas_call(
        functools.partial(surface_kernel, secs),
        out_shape=shape((secs - 1, PATCH, PATCH), f32),
        in_specs=[vmem] * (5 + secs - begin),
        out_specs=hbm,
        scratch_shapes=[
            pltpu.VMEM((secs, 2, PATCH, PATCH), f32),
            pltpu.VMEM((secs - 1, PATCH, PATCH), f32),
            pltpu.SemaphoreType.DMA((secs - 1,)),
        ],
        compiler_params=params,
        name="surface",
    )(left, right, turn, close, early, *windows[begin:])
    return (jitter, surfaces[:, None, None])


def solution(mesh):
    in_specs = (
        P(("groups", "sec"), ("tile", "row"), None),
        P(("groups", "sec"), ("tile", "row")),
        P(("groups", "sec"), None, None, None),
        P(("groups", "sec"), None, None),
        P(("tile", "row"), "groups"),
    )
    out_specs = (
        P(("groups", "sec"), ("tile", "row")),
        P("groups", ("tile", "row"), "sec", None, None),
    )
    return jax.shard_map(
        per_device, mesh=mesh, in_specs=in_specs, out_specs=out_specs, check_vma=False
    )
```

```python
import functools
import math

import jax
import jax.numpy as jnp
import numpy as np
from jax import lax
from jax.experimental import pallas as pl
from jax.experimental.pallas import tpu as pltpu
from jax.sharding import PartitionSpec as P

SEG = 512
PATCH = 128
BLOCK = 128
CAP = 2
SUB = 8
NOTE = 5
CHUNKS = (0, 2, 6, 11, 16)
PAD = 16
BANDS = ("tile", "row")


def is_pow2(n):
    return n & (n - 1) == 0


def target(me, k, n):
    return me ^ k if is_pow2(n) else (me + k) % n


def origin(me, k, n):
    return me ^ k if is_pow2(n) else (me + n - k) % n


def send(x, axis, k, n):
    return lax.ppermute(x, axis, [(i, target(i, k, n)) for i in range(n)])


def has_tail(k, n):
    return any(target(i, k, n) == (i + 1) % n for i in range(n))


def patch_order(n):
    half = n // 2
    return [0, half] + [k for k in range(n - 1, 0, -1) if k != half]


def find_slots(drift, band, owner, count):
    place = [jnp.int32(0)] * CAP
    found = jnp.int32(0)
    for p in range(count):
        hit = drift[1, band, p] == owner
        for c in range(CAP):
            place[c] = jnp.where(hit & (found == c), p, place[c])
        found = found + jnp.where(hit, 1, 0)
    return place, found


def window_place(pcol, q, slab):
    start = q * slab + pcol[0, q]
    return start >> 7, start & (BLOCK - 1)


def split(x):
    high = x.astype(jnp.bfloat16)
    return high, (x - high.astype(jnp.float32)).astype(jnp.bfloat16)


def front_kernel(owners, delay_at, drift_at, pixels, *refs):
    jitter_out, half_out, padded, first_out = refs[:4]
    messages = refs[4 : 3 + owners]
    raw, ring, wide, sums, delay, drift, loaded = refs[3 + owners :]
    rows, width = pixels.shape
    blocks = width // BLOCK
    bounds = [rows * part // 16 for part in CHUNKS]
    chunks = len(CHUNKS) - 1
    band = lax.axis_index(BANDS)

    def load(i):
        at = pl.ds(bounds[i], bounds[i + 1] - bounds[i])
        return pltpu.make_async_copy(pixels.at[at, :], raw.at[at, :], loaded.at[i])

    small = [
        pltpu.make_async_copy(a, b, loaded.at[chunks + i])
        for i, (a, b) in enumerate(((delay_at, delay), (drift_at, drift)))
    ]
    small[0].start()
    for i in range(chunks):
        load(i).start()
    small[1].start()
    padded[0] = jnp.zeros(padded.shape[1:], jnp.float32)
    padded[blocks + 1] = jnp.zeros(padded.shape[1:], jnp.float32)
    padded[1 : blocks + 1, 0:PAD, :] = jnp.zeros((blocks, PAD, BLOCK), jnp.float32)
    ring[:, 0:PAD, :] = jnp.zeros((blocks, PAD, BLOCK), jnp.float32)
    small[0].wait()
    wide[...] = jnp.broadcast_to(delay[...], (rows, rows)).T
    lane = lax.broadcasted_iota(jnp.int32, (SUB, BLOCK), 1)
    last_lane = lane == BLOCK - 1
    first_sub = lax.broadcasted_iota(jnp.int32, (SUB, BLOCK), 0) == 0
    seg = SEG // BLOCK

    def relate(at):
        here, over = pl.ds(at + PAD, SUB), pl.ds(at + (PAD - 1), SUB)
        cross = [jnp.zeros((SUB, BLOCK), jnp.float32)] * seg
        for v in range(blocks):
            i = v % seg
            x, behind = padded[v + 1, here, :], ring[v, here, :]
            top = pl.ds(at + (PAD - 1), 1)
            above = jnp.where(first_sub, padded[v + 1, top, :], pltpu.roll(x, 1, 0))
            above_behind = jnp.where(first_sub, ring[v, top, :], pltpu.roll(behind, 1, 0))
            cross[i] = cross[i] + (above * behind - above_behind * x)
        sums[0, pl.ds(at + SUB, SUB), :] = sum(cross[1:], cross[0])

    def eight_rows(g, _):
        at = pl.multiple_of(g * SUB, SUB)
        delays = wide[pl.ds(at, SUB), :]
        moved = lane + delays
        index = moved & (BLOCK - 1)
        near = moved < BLOCK
        picked = [
            jnp.take_along_axis(
                raw[pl.ds(at, SUB), v * BLOCK : (v + 1) * BLOCK],
                index,
                axis=1,
                mode="promise_in_bounds",
            )
            for v in range(blocks)
        ]
        picked.append(jnp.zeros((SUB, BLOCK), jnp.float32))
        x = [jnp.where(near, picked[v], picked[v + 1]) for v in range(blocks)]
        power = [jnp.zeros((SUB, BLOCK), jnp.float32)] * seg
        for v in range(blocks):
            prv = x[v - 1] if v % seg else x[v + seg - 1]
            padded[v + 1, pl.ds(at + PAD, SUB), :] = x[v]
            ring[v, pl.ds(at + PAD, SUB), :] = pltpu.roll(jnp.where(last_lane, prv, x[v]), 1, 1)
            power[v % seg] = power[v % seg] + x[v] * x[v]
        sums[1, pl.ds(at + SUB, SUB), :] = sum(power[1:], power[0])
        return 0

    def again(g, _):
        relate(pl.multiple_of(g * SUB, SUB))
        return 0

    for i in range(chunks):
        load(i).wait()
        groups = bounds[i] // SUB, bounds[i + 1] // SUB
        lax.fori_loop(*groups, eight_rows, 0, unroll=True)
        lax.fori_loop(*groups, again, 0, unroll=True)

    small[1].wait()
    total_cross = jnp.sum(sums[0, SUB:], axis=1, keepdims=True)
    total_power = jnp.sum(sums[1, SUB:], axis=1, keepdims=True)
    row_index = lax.broadcasted_iota(jnp.int32, (rows, BLOCK), 0)
    power = jnp.broadcast_to(total_power, (rows, BLOCK))
    power = power + jnp.where(row_index == 0, 0.0, pltpu.roll(power, 1, 0))
    cross = jnp.broadcast_to(total_cross, (rows, BLOCK))
    jitter = cross / (power + 1e-5 * 2 * (blocks // seg))
    half = 0.5 * jitter
    half_out[...] = half
    count = drift.shape[2]
    for k in range(1, owners):
        place, _ = find_slots(drift, band, target(band, k, owners), count)
        for c in range(CAP):
            messages[k - 1][c * BLOCK : (c + 1) * BLOCK, :] = corrected(
                padded, half, drift[0, band, place[c]]
            ).astype(jnp.bfloat16)
    jitter_out[...] = jitter.T[0:1, :]
    for v in range(blocks):
        first_out[0, v : v + 1, :] = padded[v + 1, PAD : PAD + 1, :]
        first_out[1, v : v + 1, :] = padded[v + 1, PAD + rows - 1 : PAD + rows, :]
    first = first_out[0].astype(jnp.bfloat16)
    last, rest = split(first_out[1])
    base = CAP * BLOCK
    for k in range(1, owners):
        message = messages[k - 1]
        message[base : base + blocks, :] = first
        message[base + blocks : base + 2 * blocks, :] = last
        if message.shape[0] > base + 2 * blocks:
            message[base + 2 * blocks : base + 3 * blocks, :] = rest


def corrected(padded, half, n):
    rows = half.shape[0]
    here = padded[n + 1, PAD : PAD + rows, :]
    lane = lax.broadcasted_iota(jnp.int32, here.shape, 1)
    left = jnp.where(lane == BLOCK - 1, padded[n, PAD : PAD + rows, :], here)
    right = jnp.where(lane == 0, padded[n + 2, PAD : PAD + rows, :], here)
    return here - half * (pltpu.roll(right, BLOCK - 1, 1) - pltpu.roll(left, 1, 1))


def plan_kernel(owners, secs, drift, weight, pcol, half_in, padded, acc, own, notes, shares):
    blocks = padded.shape[0] - 2
    slab = blocks * BLOCK // secs
    band = lax.axis_index(BANDS)
    half = half_in[...]
    lane = lax.broadcasted_iota(jnp.int32, half.shape, 1)
    place, _ = find_slots(drift, band, band, drift.shape[2])
    for c in range(CAP):
        own[c * BLOCK : (c + 1) * BLOCK, :] = corrected(
            padded, half, drift[0, band, place[c]]
        ).astype(jnp.bfloat16)
    for q in range(secs):
        n, o = window_place(pcol, q, slab)
        n1 = jnp.minimum(n + 1, blocks - 1)
        near, far = (
            corrected(padded, half, i).astype(jnp.bfloat16).astype(jnp.float32) for i in (n, n1)
        )
        picked = jnp.where(lane >= o, near, far)
        acc[q] = pltpu.roll(picked, (BLOCK - o) & (BLOCK - 1), 1)
        notes[owners * CAP * NOTE + 2 * q] = n
        notes[owners * CAP * NOTE + 2 * q + 1] = o
    for k in range(owners):
        source = origin(band, k, owners)
        place, found = find_slots(drift, source, band, drift.shape[2])
        for c in range(CAP):
            goal = drift[2, source, place[c]]
            q = goal // (slab // BLOCK)
            n, o = window_place(pcol, q, slab)
            hit = (found > c) & ((goal == n) | (goal == n + 1))
            at = (k * CAP + c) * NOTE
            notes[at] = jnp.where(hit, 1, 0)
            notes[at + 1] = q
            notes[at + 2] = o
            notes[at + 3] = jnp.where(goal == n, 1, 0)
            notes[at + 4] = drift[0, source, place[c]]
            shares[k * CAP + c] = weight[0, source, place[c]]


def row_differences(x):
    blocks = x.shape[0]
    seg = SEG // BLOCK
    lane = lax.broadcasted_iota(jnp.int32, x.shape, 1)
    block = lax.broadcasted_iota(jnp.int32, x.shape, 0)
    ahead = pltpu.roll(x, BLOCK - 1, 1)
    behind = pltpu.roll(x, 1, 1)
    last_lane = lane == BLOCK - 1
    first_sub = lax.broadcasted_iota(jnp.int32, (SUB, BLOCK), 0) == 0
    first_lane = lane == 0
    nxt = pltpu.roll(ahead, blocks - 1, 0)
    prv = pltpu.roll(behind, 1, 0)
    line = jnp.where(last_lane, jnp.where(block == blocks - 1, 0.0, nxt), ahead) - jnp.where(
        first_lane, jnp.where(block == 0, 0.0, prv), behind
    )
    nxt = jnp.where(block % seg == seg - 1, pltpu.roll(ahead, seg - 1, 0), nxt)
    prv = jnp.where(block % seg == 0, pltpu.roll(behind, blocks - seg + 1, 0), prv)
    ring = jnp.where(last_lane, nxt, ahead) - jnp.where(first_lane, prv, behind)
    return line, ring


def total(x):
    return jnp.sum(jnp.sum(x, axis=1, keepdims=True), axis=0, keepdims=True)


def blend_kernel(owners, secs, notes, shares, jitter_in, edges, begun, *refs):
    messages = refs[:owners]
    jitter_out = refs[owners]
    windows = refs[owners + 1 : owners + 1 + secs]
    firsts, lasts, tails, fixed, acc, den = refs[owners + 1 + secs :]
    blocks = edges.shape[1]
    seg = SEG // BLOCK
    band = lax.axis_index(BANDS)
    sec = lax.axis_index("sec")
    base = CAP * BLOCK
    f32 = jnp.float32
    tiny = 1e-5 * 2 * (blocks // seg)
    firsts[band] = edges[0]
    lasts[band] = edges[1]
    for k in range(1, owners):
        source = origin(band, k, owners)
        firsts[source] = messages[k][base : base + blocks, :].astype(f32)
        lasts[source] = messages[k][base + blocks : base + 2 * blocks, :].astype(f32)
        if messages[k].shape[0] > base + 2 * blocks:
            tails[source] = messages[k][base + 2 * blocks : base + 3 * blocks, :].astype(f32)

    def estimate(row, ring, above):
        return -total(above * ring) / (total(row * row + above * above) + tiny)

    own = jnp.zeros((1, 1), f32)
    for j in range(owners):
        row = firsts[j]
        line, ring = row_differences(row)
        if j == 0:
            fixed[j] = row.astype(jnp.bfloat16).astype(f32)
        else:
            above = lasts[j - 1] + jnp.where(band == j, tails[j - 1], 0.0)
            found = estimate(row, ring, above)
            own = jnp.where(band == j, found, own)
            fixed[j] = (row - 0.5 * found * line).astype(jnp.bfloat16).astype(f32)
    lane_row = lax.broadcasted_iota(jnp.int32, jitter_in.shape, 1)
    jitter_out[...] = jnp.where(lane_row == 0, own, jitter_in[...])

    top = lax.broadcasted_iota(jnp.int32, (BLOCK, BLOCK), 0) == 0
    lane1 = lax.broadcasted_iota(jnp.int32, (1, BLOCK), 1)
    acc[...] = begun[...]
    for q in range(secs):
        n = notes[owners * CAP * NOTE + 2 * q]
        o = notes[owners * CAP * NOTE + 2 * q + 1]
        n1 = jnp.minimum(n + 1, blocks - 1)
        picked = jnp.where(lane1 >= o, fixed[band, pl.ds(n, 1), :], fixed[band, pl.ds(n1, 1), :])
        picked = pltpu.roll(jnp.broadcast_to(picked, (SUB, BLOCK)), (BLOCK - o) & (BLOCK - 1), 1)
        acc[q, 0:1, :] = picked[0:1, :]
        den[q] = jnp.ones((1, BLOCK), f32)

    for k in range(owners):
        source = origin(band, k, owners)
        for c in range(CAP):
            at = (k * CAP + c) * NOTE

            @pl.when(notes[at] > 0)
            def _():
                q, o = notes[at + 1], notes[at + 2]
                w = shares[k * CAP + c]
                turn = (BLOCK - o) & (BLOCK - 1)
                picture = messages[k][c * BLOCK : (c + 1) * BLOCK, :].astype(f32)
                origin_block = notes[at + 4]
                picture = jnp.where(top, fixed[source, pl.ds(origin_block, 1), :], picture)
                inside = (lane1 + o < BLOCK) == (notes[at + 3] > 0)
                factor = jnp.where(inside, w, 0.0)
                acc[q] = acc[q] + factor * pltpu.roll(picture, turn, 1)
                den[q] = den[q] + factor

    for k in range(secs):
        q = target(sec, k, secs)
        windows[k][...] = (acc[q] * (1.0 / den[q])).astype(jnp.bfloat16)


def dot(a, b):
    return jnp.dot(a, b, preferred_element_type=jnp.float32)


def spectra(patches, left, right):
    side = PATCH
    found = []
    for at in range(0, len(patches), 2):
        pair = patches[at : at + 2]
        beside = jnp.concatenate(pair, 1) if len(pair) > 1 else pair[0]
        columns = dot(left, jnp.concatenate([beside, beside], 0))
        stack = []
        for i in range(len(pair)):
            high, low = split(columns[:, i * side : (i + 1) * side])
            stack.append(jnp.concatenate([high, low, high], 1))
        grid = dot(jnp.concatenate(stack, 0), right)
        for i in range(len(pair)):
            one = grid[2 * side * i : 2 * side * (i + 1)]
            real = one[:side, :side] - one[side:, side:]
            imag = -(one[side:, :side] + one[:side, side:])
            found.append((real, imag))
    return found


def spectrum_kernel(left, right, *refs):
    patches, out = refs[:-1], refs[-1]
    for k, (real, imag) in enumerate(spectra([p[...] for p in patches], left[...], right[...])):
        out[k, 0] = real
        out[k, 1] = imag


def surface_kernel(secs, left, right, turn, close, early, *refs):
    late = refs[: secs - early.shape[0]]
    out, freq, held, sent = refs[len(late) :]
    sec = lax.axis_index("sec")
    side = PATCH
    begun = early.shape[0]
    order = patch_order(secs)
    for k in range(begun):
        freq[origin(sec, order[k], secs)] = early[k]
    for k, (real, imag) in enumerate(spectra([p[...] for p in late], left[...], right[...])):
        at = origin(sec, order[begun + k], secs)
        freq[at, 0] = real
        freq[at, 1] = imag
    rows = []
    for s in range(secs - 1):
        real, imag = freq[s, 0], freq[s, 1]
        next_real, next_imag = freq[s + 1, 0], freq[s + 1, 1]
        cross_real = real * next_real + imag * next_imag
        cross_imag = imag * next_real - real * next_imag
        magnitude = jnp.sqrt(cross_real * cross_real + cross_imag * cross_imag)
        damping = (0.5 / (side * side)) * total(magnitude) + 1e-6
        scaled = 1.0 / (magnitude + damping)
        high, low = split(jnp.concatenate([cross_real * scaled, cross_imag * scaled], 1))
        rows.append(jnp.concatenate([high, low, high], 1))
    back = dot(jnp.concatenate(rows, 0), turn[...])
    copies = []
    for s in range(secs - 1):
        one = back[s * side : (s + 1) * side]
        high, low = split(jnp.concatenate([one[:, :side], one[:, side:]], 0))
        held[s] = dot(close[...], jnp.concatenate([high, low, high], 0))
        copies.append(pltpu.make_async_copy(held.at[s], out.at[s], sent.at[s]))
        copies[-1].start()
    for copy in copies:
        copy.wait()


def in_hbm(x):
    return pltpu.with_memory_space_constraint(x, pltpu.HBM)


def in_smem(x):
    return pltpu.with_memory_space_constraint(x, pltpu.SMEM)


def halves(x):
    high = x.astype(jnp.bfloat16)
    return high, (x - high.astype(np.float32)).astype(jnp.bfloat16)


def dft_tables(length):
    indices = np.arange(length)
    angles = (indices[:, None] * indices[None, :] % length) * (2.0 * math.pi / length)
    cosine, sine = np.cos(angles).astype(np.float32), np.sin(angles).astype(np.float32)
    left = np.concatenate(halves(np.concatenate([cosine, sine], 0)), 1)
    high, low = halves(np.concatenate([cosine, sine], 1))
    right = np.concatenate([high, high, low], 0)
    high, low = halves(
        np.concatenate(
            [np.concatenate([cosine, sine], 1), np.concatenate([-sine, cosine], 1)], 0
        )
    )
    turn = np.concatenate([high, high, low], 0)
    high, low = halves(np.concatenate([cosine, -sine], 1) / np.float32(length))
    close = np.concatenate([high, high, low], 1)
    return [jnp.asarray(t) for t in (left, right, turn, close)]


def per_device(section_pixels, jitter_index, drift_list, blend_weight, patch_col):
    pixels = section_pixels[0]
    rows, width = pixels.shape
    blocks = width // BLOCK
    owners = lax.axis_size(BANDS)
    secs = lax.axis_size("sec")
    chunks = len(CHUNKS) - 1
    drifts = jnp.transpose(drift_list[0], (2, 0, 1))
    f32, bf16 = jnp.float32, jnp.bfloat16
    vmem = pl.BlockSpec(memory_space=pltpu.VMEM)
    smem = pl.BlockSpec(memory_space=pltpu.SMEM)
    hbm = pl.BlockSpec(memory_space=pltpu.HBM)
    shape = jax.ShapeDtypeStruct
    message_rows = [
        CAP * BLOCK + (3 if has_tail(k, owners) else 2) * blocks for k in range(1, owners)
    ]
    params = pltpu.CompilerParams(vmem_limit_bytes=24 * 1024 * 1024)
    jitter, half, padded, edges, *messages = pl.pallas_call(
        functools.partial(front_kernel, owners),
        out_shape=[
            shape((1, rows), f32),
            shape((rows, BLOCK), f32),
            shape((blocks + 2, rows + PAD, BLOCK), f32),
            shape((2, blocks, BLOCK), f32),
        ]
        + [shape((r, BLOCK), bf16) for r in message_rows],
        in_specs=[hbm] * 3,
        out_specs=[vmem] * (3 + owners),
        scratch_shapes=[
            pltpu.VMEM((rows, width), f32),
            pltpu.VMEM((blocks, rows + PAD, BLOCK), f32),
            pltpu.VMEM((rows, rows), jnp.int32),
            pltpu.VMEM((2, rows + SUB, BLOCK), f32),
            pltpu.VMEM((1, rows), jnp.int32),
            pltpu.SMEM(drifts.shape, jnp.int32),
            pltpu.SemaphoreType.DMA((chunks + 2,)),
        ],
        compiler_params=params,
        name="front",
    )(*map(in_hbm, (jitter_index, drifts, pixels)))
    begun, own, notes, shares = pl.pallas_call(
        functools.partial(plan_kernel, owners, secs),
        out_shape=[
            shape((secs, PATCH, PATCH), f32),
            shape((CAP * BLOCK, BLOCK), bf16),
            pltpu.SMEM((owners * CAP * NOTE + 2 * secs,), jnp.int32),
            pltpu.SMEM((owners * CAP,), f32),
        ],
        in_specs=[smem, smem, smem, vmem, vmem],
        out_specs=[vmem, vmem, smem, smem],
        compiler_params=params,
        cost_estimate=pl.CostEstimate(flops=10**8, bytes_accessed=10**6, transcendentals=0),
        name="plan",
    )(drifts, blend_weight, patch_col, half, padded)
    messages = [own] + [send(messages[k - 1], BANDS, k, owners) for k in range(1, owners)]
    jitter, *windows = pl.pallas_call(
        functools.partial(blend_kernel, owners, secs),
        out_shape=[shape((1, rows), f32)] + [shape((PATCH, PATCH), bf16)] * secs,
        in_specs=[smem, smem] + [vmem] * (3 + owners),
        out_specs=[vmem] * (1 + secs),
        scratch_shapes=[pltpu.VMEM((owners, blocks, BLOCK), f32)] * 4
        + [pltpu.VMEM((secs, PATCH, PATCH), f32), pltpu.VMEM((secs, 1, PATCH), f32)],
        compiler_params=params,
        name="blend",
    )(in_smem(notes), in_smem(shares), jitter, edges, begun, *messages)
    order = patch_order(secs)
    windows = windows[:1] + [send(windows[k], "sec", k, secs) for k in order[1:]]
    left, right, turn, close = dft_tables(PATCH)
    begin = secs // 2
    early = pl.pallas_call(
        spectrum_kernel,
        out_shape=shape((begin, 2, PATCH, PATCH), f32),
        in_specs=[vmem] * (2 + begin),
        out_specs=vmem,
        compiler_params=params,
        cost_estimate=pl.CostEstimate(flops=10**8, bytes_accessed=10**6, transcendentals=0),
        name="spectrum",
    )(left, right, *windows[:begin])
    surfaces = pl.pallas_call(
        functools.partial(surface_kernel, secs),
        out_shape=shape((secs - 1, PATCH, PATCH), f32),
        in_specs=[vmem] * (5 + secs - begin),
        out_specs=hbm,
        scratch_shapes=[
            pltpu.VMEM((secs, 2, PATCH, PATCH), f32),
            pltpu.VMEM((secs - 1, PATCH, PATCH), f32),
            pltpu.SemaphoreType.DMA((secs - 1,)),
        ],
        compiler_params=params,
        name="surface",
    )(left, right, turn, close, early, *windows[begin:])
    return (jitter, surfaces[:, None, None])


def solution(mesh):
    in_specs = (
        P(("groups", "sec"), ("tile", "row"), None),
        P(("groups", "sec"), ("tile", "row")),
        P(("groups", "sec"), None, None, None),
        P(("groups", "sec"), None, None),
        P(("tile", "row"), "groups"),
    )
    out_specs = (
        P(("groups", "sec"), ("tile", "row")),
        P("groups", ("tile", "row"), "sec", None, None),
    )
    return jax.shard_map(
        per_device, mesh=mesh, in_specs=in_specs, out_specs=out_specs, check_vma=False
    )
```

```python
import functools
import math

import jax
import jax.numpy as jnp
import numpy as np
from jax import lax
from jax.experimental import pallas as pl
from jax.experimental.pallas import tpu as pltpu
from jax.sharding import PartitionSpec as P

SEG = 512
PATCH = 128
BLOCK = 128
CAP = 2
SUB = 8
NOTE = 5
CHUNKS = (0, 2, 6, 11, 16)
PAD = 16
BANDS = ("tile", "row")


def is_pow2(n):
    return n & (n - 1) == 0


def target(me, k, n):
    return me ^ k if is_pow2(n) else (me + k) % n


def origin(me, k, n):
    return me ^ k if is_pow2(n) else (me + n - k) % n


def send(x, axis, k, n):
    return lax.ppermute(x, axis, [(i, target(i, k, n)) for i in range(n)])


def has_tail(k, n):
    return any(target(i, k, n) == (i + 1) % n for i in range(n))


def patch_order(n):
    half = n // 2
    return [0, half] + [k for k in range(n - 1, 0, -1) if k != half]


def find_slots(drift, band, owner, count):
    place = [jnp.int32(0)] * CAP
    found = jnp.int32(0)
    for p in range(count):
        hit = drift[1, band, p] == owner
        for c in range(CAP):
            place[c] = jnp.where(hit & (found == c), p, place[c])
        found = found + jnp.where(hit, 1, 0)
    return place, found


def window_place(pcol, q, slab):
    start = q * slab + pcol[0, q]
    return start >> 7, start & (BLOCK - 1)


def split(x):
    high = x.astype(jnp.bfloat16)
    return high, (x - high.astype(jnp.float32)).astype(jnp.bfloat16)


def front_kernel(owners, delay_at, drift_at, pixels, *refs):
    jitter_out, half_out, padded, first_out = refs[:4]
    messages = refs[4 : 3 + owners]
    raw, ring, wide, sums, delay, drift, loaded = refs[3 + owners :]
    rows, width = pixels.shape
    blocks = width // BLOCK
    bounds = [rows * part // 16 for part in CHUNKS]
    chunks = len(CHUNKS) - 1
    band = lax.axis_index(BANDS)

    def load(i):
        at = pl.ds(bounds[i], bounds[i + 1] - bounds[i])
        return pltpu.make_async_copy(pixels.at[at, :], raw.at[at, :], loaded.at[i])

    small = [
        pltpu.make_async_copy(a, b, loaded.at[chunks + i])
        for i, (a, b) in enumerate(((delay_at, delay), (drift_at, drift)))
    ]
    small[0].start()
    for i in range(chunks):
        load(i).start()
    small[1].start()
    padded[0] = jnp.zeros(padded.shape[1:], jnp.float32)
    padded[blocks + 1] = jnp.zeros(padded.shape[1:], jnp.float32)
    padded[1 : blocks + 1, 0:PAD, :] = jnp.zeros((blocks, PAD, BLOCK), jnp.float32)
    ring[:, 0:PAD, :] = jnp.zeros((blocks, PAD, BLOCK), jnp.float32)
    small[0].wait()
    wide[...] = jnp.broadcast_to(delay[...], (rows, rows)).T
    lane = lax.broadcasted_iota(jnp.int32, (SUB, BLOCK), 1)
    last_lane = lane == BLOCK - 1
    first_sub = lax.broadcasted_iota(jnp.int32, (SUB, BLOCK), 0) == 0
    seg = SEG // BLOCK

    def relate(at):
        here, over = pl.ds(at + PAD, SUB), pl.ds(at + (PAD - 1), SUB)
        cross = [jnp.zeros((SUB, BLOCK), jnp.float32)] * seg
        for v in range(blocks):
            i = v % seg
            x, behind = padded[v + 1, here, :], ring[v, here, :]
            top = pl.ds(at + (PAD - 1), 1)
            above = jnp.where(first_sub, padded[v + 1, top, :], pltpu.roll(x, 1, 0))
            above_behind = jnp.where(first_sub, ring[v, top, :], pltpu.roll(behind, 1, 0))
            cross[i] = cross[i] + (above * behind - above_behind * x)
        sums[0, pl.ds(at + SUB, SUB), :] = sum(cross[1:], cross[0])

    def eight_rows(g, _):
        at = pl.multiple_of(g * SUB, SUB)
        delays = wide[pl.ds(at, SUB), :]
        moved = lane + delays
        index = moved & (BLOCK - 1)
        near = moved < BLOCK
        picked = [
            jnp.take_along_axis(
                raw[pl.ds(at, SUB), v * BLOCK : (v + 1) * BLOCK],
                index,
                axis=1,
                mode="promise_in_bounds",
            )
            for v in range(blocks)
        ]
        picked.append(jnp.zeros((SUB, BLOCK), jnp.float32))
        x = [jnp.where(near, picked[v], picked[v + 1]) for v in range(blocks)]
        power = [jnp.zeros((SUB, BLOCK), jnp.float32)] * seg
        for v in range(blocks):
            prv = x[v - 1] if v % seg else x[v + seg - 1]
            padded[v + 1, pl.ds(at + PAD, SUB), :] = x[v]
            ring[v, pl.ds(at + PAD, SUB), :] = pltpu.roll(jnp.where(last_lane, prv, x[v]), 1, 1)
            power[v % seg] = power[v % seg] + x[v] * x[v]
        sums[1, pl.ds(at + SUB, SUB), :] = sum(power[1:], power[0])
        return 0

    def again(g, _):
        relate(pl.multiple_of(g * SUB, SUB))
        return 0

    for i in range(chunks):
        load(i).wait()
        groups = bounds[i] // SUB, bounds[i + 1] // SUB
        lax.fori_loop(*groups, eight_rows, 0, unroll=True)
        lax.fori_loop(*groups, again, 0, unroll=True)

    small[1].wait()
    total_cross = jnp.sum(sums[0, SUB:], axis=1, keepdims=True)
    total_power = jnp.sum(sums[1, SUB:], axis=1, keepdims=True)
    row_index = lax.broadcasted_iota(jnp.int32, (rows, BLOCK), 0)
    power = jnp.broadcast_to(total_power, (rows, BLOCK))
    power = power + jnp.where(row_index == 0, 0.0, pltpu.roll(power, 1, 0))
    cross = jnp.broadcast_to(total_cross, (rows, BLOCK))
    jitter = cross / (power + 1e-5 * 2 * (blocks // seg))
    half = 0.5 * jitter
    half_out[...] = half
    count = drift.shape[2]
    for k in range(1, owners):
        place, _ = find_slots(drift, band, target(band, k, owners), count)
        for c in range(CAP):
            messages[k - 1][c * BLOCK : (c + 1) * BLOCK, :] = corrected(
                padded, half, drift[0, band, place[c]]
            ).astype(jnp.bfloat16)
    jitter_out[...] = jitter.T[0:1, :]
    for v in range(blocks):
        first_out[0, v : v + 1, :] = padded[v + 1, PAD : PAD + 1, :]
        first_out[1, v : v + 1, :] = padded[v + 1, PAD + rows - 1 : PAD + rows, :]
    first = first_out[0].astype(jnp.bfloat16)
    last, rest = split(first_out[1])
    base = CAP * BLOCK
    for k in range(1, owners):
        message = messages[k - 1]
        message[base : base + blocks, :] = first
        message[base + blocks : base + 2 * blocks, :] = last
        if message.shape[0] > base + 2 * blocks:
            message[base + 2 * blocks : base + 3 * blocks, :] = rest


def corrected(padded, half, n):
    rows = half.shape[0]
    here = padded[n + 1, PAD : PAD + rows, :]
    lane = lax.broadcasted_iota(jnp.int32, here.shape, 1)
    left = jnp.where(lane == BLOCK - 1, padded[n, PAD : PAD + rows, :], here)
    right = jnp.where(lane == 0, padded[n + 2, PAD : PAD + rows, :], here)
    return here - half * (pltpu.roll(right, BLOCK - 1, 1) - pltpu.roll(left, 1, 1))


def plan_kernel(owners, secs, drift_at, weight_at, pcol_at, tables_at, half_in, padded, *refs):
    acc, own, notes, shares = refs[:4]
    drift, weight, pcol, tables, loaded = refs[8:]
    copies = [
        pltpu.make_async_copy(a, b, loaded.at[i])
        for i, (a, b) in enumerate(
            ((drift_at, drift), (weight_at, weight), (pcol_at, pcol), (tables_at, tables))
        )
    ]
    for copy in copies:
        copy.start()
    for copy in copies:
        copy.wait()
    fill_tables(tables, *refs[4:8])
    blocks = padded.shape[0] - 2
    slab = blocks * BLOCK // secs
    band = lax.axis_index(BANDS)
    half = half_in[...]
    lane = lax.broadcasted_iota(jnp.int32, half.shape, 1)
    place, _ = find_slots(drift, band, band, drift.shape[2])
    for c in range(CAP):
        own[c * BLOCK : (c + 1) * BLOCK, :] = corrected(
            padded, half, drift[0, band, place[c]]
        ).astype(jnp.bfloat16)
    for q in range(secs):
        n, o = window_place(pcol, q, slab)
        n1 = jnp.minimum(n + 1, blocks - 1)
        near, far = (
            corrected(padded, half, i).astype(jnp.bfloat16).astype(jnp.float32) for i in (n, n1)
        )
        picked = jnp.where(lane >= o, near, far)
        acc[q] = pltpu.roll(picked, (BLOCK - o) & (BLOCK - 1), 1)
        notes[owners * CAP * NOTE + 2 * q] = n
        notes[owners * CAP * NOTE + 2 * q + 1] = o
    for k in range(owners):
        source = origin(band, k, owners)
        place, found = find_slots(drift, source, band, drift.shape[2])
        for c in range(CAP):
            goal = drift[2, source, place[c]]
            q = goal // (slab // BLOCK)
            n, o = window_place(pcol, q, slab)
            hit = (found > c) & ((goal == n) | (goal == n + 1))
            at = (k * CAP + c) * NOTE
            notes[at] = jnp.where(hit, 1, 0)
            notes[at + 1] = q
            notes[at + 2] = o
            notes[at + 3] = jnp.where(goal == n, 1, 0)
            notes[at + 4] = drift[0, source, place[c]]
            shares[k * CAP + c] = weight[0, source, place[c]]


def row_differences(x):
    blocks = x.shape[0]
    seg = SEG // BLOCK
    lane = lax.broadcasted_iota(jnp.int32, x.shape, 1)
    block = lax.broadcasted_iota(jnp.int32, x.shape, 0)
    ahead = pltpu.roll(x, BLOCK - 1, 1)
    behind = pltpu.roll(x, 1, 1)
    last_lane = lane == BLOCK - 1
    first_sub = lax.broadcasted_iota(jnp.int32, (SUB, BLOCK), 0) == 0
    first_lane = lane == 0
    nxt = pltpu.roll(ahead, blocks - 1, 0)
    prv = pltpu.roll(behind, 1, 0)
    line = jnp.where(last_lane, jnp.where(block == blocks - 1, 0.0, nxt), ahead) - jnp.where(
        first_lane, jnp.where(block == 0, 0.0, prv), behind
    )
    nxt = jnp.where(block % seg == seg - 1, pltpu.roll(ahead, seg - 1, 0), nxt)
    prv = jnp.where(block % seg == 0, pltpu.roll(behind, blocks - seg + 1, 0), prv)
    ring = jnp.where(last_lane, nxt, ahead) - jnp.where(first_lane, prv, behind)
    return line, ring


def total(x):
    return jnp.sum(jnp.sum(x, axis=1, keepdims=True), axis=0, keepdims=True)


def blend_kernel(owners, secs, notes, shares, jitter_in, edges, begun, *refs):
    messages = refs[:owners]
    jitter_out = refs[owners]
    windows = refs[owners + 1 : owners + 1 + secs]
    firsts, lasts, tails, fixed, acc, den = refs[owners + 1 + secs :]
    blocks = edges.shape[1]
    seg = SEG // BLOCK
    band = lax.axis_index(BANDS)
    sec = lax.axis_index("sec")
    base = CAP * BLOCK
    f32 = jnp.float32
    tiny = 1e-5 * 2 * (blocks // seg)
    firsts[band] = edges[0]
    lasts[band] = edges[1]
    for k in range(1, owners):
        source = origin(band, k, owners)
        firsts[source] = messages[k][base : base + blocks, :].astype(f32)
        lasts[source] = messages[k][base + blocks : base + 2 * blocks, :].astype(f32)
        if messages[k].shape[0] > base + 2 * blocks:
            tails[source] = messages[k][base + 2 * blocks : base + 3 * blocks, :].astype(f32)

    def estimate(row, ring, above):
        return -total(above * ring) / (total(row * row + above * above) + tiny)

    own = jnp.zeros((1, 1), f32)
    for j in range(owners):
        row = firsts[j]
        line, ring = row_differences(row)
        if j == 0:
            fixed[j] = row.astype(jnp.bfloat16).astype(f32)
        else:
            above = lasts[j - 1] + jnp.where(band == j, tails[j - 1], 0.0)
            found = estimate(row, ring, above)
            own = jnp.where(band == j, found, own)
            fixed[j] = (row - 0.5 * found * line).astype(jnp.bfloat16).astype(f32)
    lane_row = lax.broadcasted_iota(jnp.int32, jitter_in.shape, 1)
    jitter_out[...] = jnp.where(lane_row == 0, own, jitter_in[...])

    top = lax.broadcasted_iota(jnp.int32, (BLOCK, BLOCK), 0) == 0
    lane1 = lax.broadcasted_iota(jnp.int32, (1, BLOCK), 1)
    acc[...] = begun[...]
    for q in range(secs):
        n = notes[owners * CAP * NOTE + 2 * q]
        o = notes[owners * CAP * NOTE + 2 * q + 1]
        n1 = jnp.minimum(n + 1, blocks - 1)
        picked = jnp.where(lane1 >= o, fixed[band, pl.ds(n, 1), :], fixed[band, pl.ds(n1, 1), :])
        picked = pltpu.roll(jnp.broadcast_to(picked, (SUB, BLOCK)), (BLOCK - o) & (BLOCK - 1), 1)
        acc[q, 0:1, :] = picked[0:1, :]
        den[q] = jnp.ones((1, BLOCK), f32)

    for k in range(owners):
        source = origin(band, k, owners)
        for c in range(CAP):
            at = (k * CAP + c) * NOTE

            @pl.when(notes[at] > 0)
            def _():
                q, o = notes[at + 1], notes[at + 2]
                w = shares[k * CAP + c]
                turn = (BLOCK - o) & (BLOCK - 1)
                picture = messages[k][c * BLOCK : (c + 1) * BLOCK, :].astype(f32)
                origin_block = notes[at + 4]
                picture = jnp.where(top, fixed[source, pl.ds(origin_block, 1), :], picture)
                inside = (lane1 + o < BLOCK) == (notes[at + 3] > 0)
                factor = jnp.where(inside, w, 0.0)
                acc[q] = acc[q] + factor * pltpu.roll(picture, turn, 1)
                den[q] = den[q] + factor

    for k in range(secs):
        q = target(sec, k, secs)
        windows[k][...] = (acc[q] * (1.0 / den[q])).astype(jnp.bfloat16)


def dot(a, b):
    return jnp.dot(a, b, preferred_element_type=jnp.float32)


def spectra(patches, left, right):
    side = PATCH
    found = []
    for at in range(0, len(patches), 2):
        pair = patches[at : at + 2]
        beside = jnp.concatenate(pair, 1) if len(pair) > 1 else pair[0]
        columns = dot(left, jnp.concatenate([beside, beside], 0))
        stack = []
        for i in range(len(pair)):
            high, low = split(columns[:, i * side : (i + 1) * side])
            stack.append(jnp.concatenate([high, low, high], 1))
        grid = dot(jnp.concatenate(stack, 0), right)
        for i in range(len(pair)):
            one = grid[2 * side * i : 2 * side * (i + 1)]
            real = one[:side, :side] - one[side:, side:]
            imag = -(one[side:, :side] + one[:side, side:])
            found.append((real, imag))
    return found


def spectrum_kernel(left, right, *refs):
    patches, out = refs[:-1], refs[-1]
    for k, (real, imag) in enumerate(spectra([p[...] for p in patches], left[...], right[...])):
        out[k, 0] = real
        out[k, 1] = imag


def surface_kernel(secs, left, right, turn, close, early, *refs):
    late = refs[: secs - early.shape[0]]
    out, freq, held, sent = refs[len(late) :]
    sec = lax.axis_index("sec")
    side = PATCH
    begun = early.shape[0]
    order = patch_order(secs)
    for k in range(begun):
        freq[origin(sec, order[k], secs)] = early[k]
    for k, (real, imag) in enumerate(spectra([p[...] for p in late], left[...], right[...])):
        at = origin(sec, order[begun + k], secs)
        freq[at, 0] = real
        freq[at, 1] = imag
    rows = []
    for s in range(secs - 1):
        real, imag = freq[s, 0], freq[s, 1]
        next_real, next_imag = freq[s + 1, 0], freq[s + 1, 1]
        cross_real = real * next_real + imag * next_imag
        cross_imag = imag * next_real - real * next_imag
        magnitude = jnp.sqrt(cross_real * cross_real + cross_imag * cross_imag)
        damping = (0.5 / (side * side)) * total(magnitude) + 1e-6
        scaled = 1.0 / (magnitude + damping)
        high, low = split(jnp.concatenate([cross_real * scaled, cross_imag * scaled], 1))
        rows.append(jnp.concatenate([high, low, high], 1))
    back = dot(jnp.concatenate(rows, 0), turn[...])
    copies = []
    for s in range(secs - 1):
        one = back[s * side : (s + 1) * side]
        high, low = split(jnp.concatenate([one[:, :side], one[:, side:]], 0))
        held[s] = dot(close[...], jnp.concatenate([high, low, high], 0))
        copies.append(pltpu.make_async_copy(held.at[s], out.at[s], sent.at[s]))
        copies[-1].start()
    for copy in copies:
        copy.wait()


def in_hbm(x):
    return pltpu.with_memory_space_constraint(x, pltpu.HBM)


def in_smem(x):
    return pltpu.with_memory_space_constraint(x, pltpu.SMEM)


def halves(x):
    high = x.astype(jnp.bfloat16)
    return high, (x - high.astype(np.float32)).astype(jnp.bfloat16)


def dft_tables(length):
    indices = np.arange(length)
    angles = (indices[:, None] * indices[None, :] % length) * (2.0 * math.pi / length)
    tables = np.concatenate([np.cos(angles), np.sin(angles)], 1).astype(np.float32)
    return jnp.asarray(np.concatenate(halves(tables), 1))


def fill_tables(tables, left, right, turn, close):
    side = PATCH
    parts = [tables[:, i * side : (i + 1) * side] for i in range(4)]
    for part, (cosine, sine) in enumerate((parts[:2], parts[2:])):
        left[:side, part * side : (part + 1) * side] = cosine
        left[side:, part * side : (part + 1) * side] = sine
        for at in (0, 1) if part == 0 else (2,):
            right[at * side : (at + 1) * side, :side] = cosine
            right[at * side : (at + 1) * side, side:] = sine
            rows = 2 * side * at
            turn[rows : rows + side, :side] = cosine
            turn[rows : rows + side, side:] = sine
            turn[rows + side : rows + 2 * side, :side] = -sine
            turn[rows + side : rows + 2 * side, side:] = cosine
            close[:, rows : rows + side] = cosine * (1.0 / side)
            close[:, rows + side : rows + 2 * side] = -sine * (1.0 / side)


def per_device(section_pixels, jitter_index, drift_list, blend_weight, patch_col):
    pixels = section_pixels[0]
    rows, width = pixels.shape
    blocks = width // BLOCK
    owners = lax.axis_size(BANDS)
    secs = lax.axis_size("sec")
    chunks = len(CHUNKS) - 1
    drifts = jnp.transpose(drift_list[0], (2, 0, 1))
    f32, bf16 = jnp.float32, jnp.bfloat16
    vmem = pl.BlockSpec(memory_space=pltpu.VMEM)
    smem = pl.BlockSpec(memory_space=pltpu.SMEM)
    hbm = pl.BlockSpec(memory_space=pltpu.HBM)
    shape = jax.ShapeDtypeStruct
    message_rows = [
        CAP * BLOCK + (3 if has_tail(k, owners) else 2) * blocks for k in range(1, owners)
    ]
    params = pltpu.CompilerParams(vmem_limit_bytes=24 * 1024 * 1024)
    jitter, half, padded, edges, *messages = pl.pallas_call(
        functools.partial(front_kernel, owners),
        out_shape=[
            shape((1, rows), f32),
            shape((rows, BLOCK), f32),
            shape((blocks + 2, rows + PAD, BLOCK), f32),
            shape((2, blocks, BLOCK), f32),
        ]
        + [shape((r, BLOCK), bf16) for r in message_rows],
        in_specs=[hbm] * 3,
        out_specs=[vmem] * (3 + owners),
        scratch_shapes=[
            pltpu.VMEM((rows, width), f32),
            pltpu.VMEM((blocks, rows + PAD, BLOCK), f32),
            pltpu.VMEM((rows, rows), jnp.int32),
            pltpu.VMEM((2, rows + SUB, BLOCK), f32),
            pltpu.VMEM((1, rows), jnp.int32),
            pltpu.SMEM(drifts.shape, jnp.int32),
            pltpu.SemaphoreType.DMA((chunks + 2,)),
        ],
        compiler_params=params,
        name="front",
    )(*map(in_hbm, (jitter_index, drifts, pixels)))
    begun, own, notes, shares, left, right, turn, close = pl.pallas_call(
        functools.partial(plan_kernel, owners, secs),
        out_shape=[
            shape((secs, PATCH, PATCH), f32),
            shape((CAP * BLOCK, BLOCK), bf16),
            pltpu.SMEM((owners * CAP * NOTE + 2 * secs,), jnp.int32),
            pltpu.SMEM((owners * CAP,), f32),
            shape((2 * PATCH, 2 * PATCH), bf16),
            shape((3 * PATCH, 2 * PATCH), bf16),
            shape((6 * PATCH, 2 * PATCH), bf16),
            shape((PATCH, 6 * PATCH), bf16),
        ],
        in_specs=[hbm] * 4 + [vmem] * 2,
        out_specs=[vmem, vmem, smem, smem] + [vmem] * 4,
        scratch_shapes=[
            pltpu.SMEM(drifts.shape, jnp.int32),
            pltpu.SMEM(blend_weight.shape, f32),
            pltpu.SMEM(patch_col.shape, jnp.int32),
            pltpu.VMEM((PATCH, 4 * PATCH), bf16),
            pltpu.SemaphoreType.DMA((4,)),
        ],
        compiler_params=params,
        cost_estimate=pl.CostEstimate(flops=10**8, bytes_accessed=10**6, transcendentals=0),
        name="plan",
    )(*map(in_hbm, (drifts, blend_weight, patch_col, dft_tables(PATCH))), half, padded)
    messages = [own] + [send(messages[k - 1], BANDS, k, owners) for k in range(1, owners)]
    jitter, *windows = pl.pallas_call(
        functools.partial(blend_kernel, owners, secs),
        out_shape=[shape((1, rows), f32)] + [shape((PATCH, PATCH), bf16)] * secs,
        in_specs=[smem, smem] + [vmem] * (3 + owners),
        out_specs=[vmem] * (1 + secs),
        scratch_shapes=[pltpu.VMEM((owners, blocks, BLOCK), f32)] * 4
        + [pltpu.VMEM((secs, PATCH, PATCH), f32), pltpu.VMEM((secs, 1, PATCH), f32)],
        compiler_params=params,
        name="blend",
    )(in_smem(notes), in_smem(shares), jitter, edges, begun, *messages)
    order = patch_order(secs)
    windows = windows[:1] + [send(windows[k], "sec", k, secs) for k in order[1:]]
    begin = secs // 2
    early = pl.pallas_call(
        spectrum_kernel,
        out_shape=shape((begin, 2, PATCH, PATCH), f32),
        in_specs=[vmem] * (2 + begin),
        out_specs=vmem,
        compiler_params=params,
        cost_estimate=pl.CostEstimate(flops=10**8, bytes_accessed=10**6, transcendentals=0),
        name="spectrum",
    )(left, right, *windows[:begin])
    surfaces = pl.pallas_call(
        functools.partial(surface_kernel, secs),
        out_shape=shape((secs - 1, PATCH, PATCH), f32),
        in_specs=[vmem] * (5 + secs - begin),
        out_specs=hbm,
        scratch_shapes=[
            pltpu.VMEM((secs, 2, PATCH, PATCH), f32),
            pltpu.VMEM((secs - 1, PATCH, PATCH), f32),
            pltpu.SemaphoreType.DMA((secs - 1,)),
        ],
        compiler_params=params,
        name="surface",
    )(left, right, turn, close, early, *windows[begin:])
    return (jitter, surfaces[:, None, None])


def solution(mesh):
    in_specs = (
        P(("groups", "sec"), ("tile", "row"), None),
        P(("groups", "sec"), ("tile", "row")),
        P(("groups", "sec"), None, None, None),
        P(("groups", "sec"), None, None),
        P(("tile", "row"), "groups"),
    )
    out_specs = (
        P(("groups", "sec"), ("tile", "row")),
        P("groups", ("tile", "row"), "sec", None, None),
    )
    return jax.shard_map(
        per_device, mesh=mesh, in_specs=in_specs, out_specs=out_specs, check_vma=False
    )
```

```python
import functools
import math

import jax
import jax.numpy as jnp
import numpy as np
from jax import lax
from jax.experimental import pallas as pl
from jax.experimental.pallas import tpu as pltpu
from jax.sharding import PartitionSpec as P

SEG = 512
PATCH = 128
BLOCK = 128
CAP = 2
SUB = 8
NOTE = 5
CHUNKS = (0, 2, 6, 11, 16)
PAD = 16
BANDS = ("tile", "row")


def is_pow2(n):
    return n & (n - 1) == 0


def target(me, k, n):
    return me ^ k if is_pow2(n) else (me + k) % n


def origin(me, k, n):
    return me ^ k if is_pow2(n) else (me + n - k) % n


def send(x, axis, k, n):
    return lax.ppermute(x, axis, [(i, target(i, k, n)) for i in range(n)])


def has_tail(k, n):
    return any(target(i, k, n) == (i + 1) % n for i in range(n))


def patch_order(n):
    half = n // 2
    return [0, half] + [k for k in range(n - 1, 0, -1) if k != half]


def find_slots(drift, band, owner, count):
    place = [jnp.int32(0)] * CAP
    found = jnp.int32(0)
    for p in range(count):
        hit = drift[1, band, p] == owner
        for c in range(CAP):
            place[c] = jnp.where(hit & (found == c), p, place[c])
        found = found + jnp.where(hit, 1, 0)
    return place, found


def window_place(pcol, q, slab):
    start = q * slab + pcol[0, q]
    return start >> 7, start & (BLOCK - 1)


def split(x):
    high = x.astype(jnp.bfloat16)
    return high, (x - high.astype(jnp.float32)).astype(jnp.bfloat16)


def front_kernel(owners, delay_at, drift_at, pixels, *refs):
    half_out, padded, first_out = refs[:3]
    messages = refs[3 : 2 + owners]
    raw, ring, wide, sums, delay, drift, loaded = refs[2 + owners :]
    rows, width = pixels.shape
    blocks = width // BLOCK
    bounds = [rows * part // 16 for part in CHUNKS]
    chunks = len(CHUNKS) - 1
    band = lax.axis_index(BANDS)

    def load(i):
        at = pl.ds(bounds[i], bounds[i + 1] - bounds[i])
        return pltpu.make_async_copy(pixels.at[at, :], raw.at[at, :], loaded.at[i])

    small = [
        pltpu.make_async_copy(a, b, loaded.at[chunks + i])
        for i, (a, b) in enumerate(((delay_at, delay), (drift_at, drift)))
    ]
    small[0].start()
    for i in range(chunks):
        load(i).start()
    small[1].start()
    padded[0] = jnp.zeros(padded.shape[1:], jnp.float32)
    padded[blocks + 1] = jnp.zeros(padded.shape[1:], jnp.float32)
    padded[1 : blocks + 1, 0:PAD, :] = jnp.zeros((blocks, PAD, BLOCK), jnp.float32)
    ring[:, 0:PAD, :] = jnp.zeros((blocks, PAD, BLOCK), jnp.float32)
    small[0].wait()
    wide[...] = jnp.broadcast_to(delay[...], (rows, rows)).T
    lane = lax.broadcasted_iota(jnp.int32, (SUB, BLOCK), 1)
    last_lane = lane == BLOCK - 1
    first_sub = lax.broadcasted_iota(jnp.int32, (SUB, BLOCK), 0) == 0
    seg = SEG // BLOCK

    def relate(at):
        here, over = pl.ds(at + PAD, SUB), pl.ds(at + (PAD - 1), SUB)
        cross = [jnp.zeros((SUB, BLOCK), jnp.float32)] * seg
        for v in range(blocks):
            i = v % seg
            x, behind = padded[v + 1, here, :], ring[v, here, :]
            top = pl.ds(at + (PAD - 1), 1)
            above = jnp.where(first_sub, padded[v + 1, top, :], pltpu.roll(x, 1, 0))
            above_behind = jnp.where(first_sub, ring[v, top, :], pltpu.roll(behind, 1, 0))
            cross[i] = cross[i] + (above * behind - above_behind * x)
        sums[0, pl.ds(at + SUB, SUB), :] = sum(cross[1:], cross[0])

    def eight_rows(g, _):
        at = pl.multiple_of(g * SUB, SUB)
        delays = wide[pl.ds(at, SUB), :]
        moved = lane + delays
        index = moved & (BLOCK - 1)
        near = moved < BLOCK
        picked = [
            jnp.take_along_axis(
                raw[pl.ds(at, SUB), v * BLOCK : (v + 1) * BLOCK],
                index,
                axis=1,
                mode="promise_in_bounds",
            )
            for v in range(blocks)
        ]
        picked.append(jnp.zeros((SUB, BLOCK), jnp.float32))
        x = [jnp.where(near, picked[v], picked[v + 1]) for v in range(blocks)]
        power = [jnp.zeros((SUB, BLOCK), jnp.float32)] * seg
        for v in range(blocks):
            prv = x[v - 1] if v % seg else x[v + seg - 1]
            padded[v + 1, pl.ds(at + PAD, SUB), :] = x[v]
            ring[v, pl.ds(at + PAD, SUB), :] = pltpu.roll(jnp.where(last_lane, prv, x[v]), 1, 1)
            power[v % seg] = power[v % seg] + x[v] * x[v]
        sums[1, pl.ds(at + SUB, SUB), :] = sum(power[1:], power[0])
        return 0

    def again(g, _):
        relate(pl.multiple_of(g * SUB, SUB))
        return 0

    for i in range(chunks):
        load(i).wait()
        groups = bounds[i] // SUB, bounds[i + 1] // SUB
        lax.fori_loop(*groups, eight_rows, 0, unroll=True)
        lax.fori_loop(*groups, again, 0, unroll=True)

    small[1].wait()
    total_cross = jnp.sum(sums[0, SUB:], axis=1, keepdims=True)
    total_power = jnp.sum(sums[1, SUB:], axis=1, keepdims=True)
    row_index = lax.broadcasted_iota(jnp.int32, (rows, BLOCK), 0)
    power = jnp.broadcast_to(total_power, (rows, BLOCK))
    power = power + jnp.where(row_index == 0, 0.0, pltpu.roll(power, 1, 0))
    cross = jnp.broadcast_to(total_cross, (rows, BLOCK))
    jitter = cross / (power + 1e-5 * 2 * (blocks // seg))
    half = 0.5 * jitter
    half_out[...] = half
    count = drift.shape[2]
    for k in range(1, owners):
        place, _ = find_slots(drift, band, target(band, k, owners), count)
        for c in range(CAP):
            messages[k - 1][c * BLOCK : (c + 1) * BLOCK, :] = corrected(
                padded, half, drift[0, band, place[c]]
            ).astype(jnp.bfloat16)
    for v in range(blocks):
        first_out[0, v : v + 1, :] = padded[v + 1, PAD : PAD + 1, :]
        first_out[1, v : v + 1, :] = padded[v + 1, PAD + rows - 1 : PAD + rows, :]
    first = first_out[0].astype(jnp.bfloat16)
    last, rest = split(first_out[1])
    base = CAP * BLOCK
    for k in range(1, owners):
        message = messages[k - 1]
        message[base : base + blocks, :] = first
        message[base + blocks : base + 2 * blocks, :] = last
        if message.shape[0] > base + 2 * blocks:
            message[base + 2 * blocks : base + 3 * blocks, :] = rest


def corrected(padded, half, n):
    rows = half.shape[0]
    here = padded[n + 1, PAD : PAD + rows, :]
    lane = lax.broadcasted_iota(jnp.int32, here.shape, 1)
    left = jnp.where(lane == BLOCK - 1, padded[n, PAD : PAD + rows, :], here)
    right = jnp.where(lane == 0, padded[n + 2, PAD : PAD + rows, :], here)
    return here - half * (pltpu.roll(right, BLOCK - 1, 1) - pltpu.roll(left, 1, 1))


def plan_kernel(owners, secs, drift_at, weight_at, pcol_at, tables_at, half_in, padded, *refs):
    acc, own, notes, shares = refs[:4]
    jitter_out, drift, weight, pcol, tables, loaded = refs[8:]
    copies = [
        pltpu.make_async_copy(a, b, loaded.at[i])
        for i, (a, b) in enumerate(
            ((drift_at, drift), (weight_at, weight), (pcol_at, pcol), (tables_at, tables))
        )
    ]
    for copy in copies:
        copy.start()
    for copy in copies:
        copy.wait()
    fill_tables(tables, *refs[4:8])
    blocks = padded.shape[0] - 2
    slab = blocks * BLOCK // secs
    band = lax.axis_index(BANDS)
    half = half_in[...]
    jitter_out[...] = (2.0 * half).T[0:1, :]
    lane = lax.broadcasted_iota(jnp.int32, half.shape, 1)
    place, _ = find_slots(drift, band, band, drift.shape[2])
    for c in range(CAP):
        own[c * BLOCK : (c + 1) * BLOCK, :] = corrected(
            padded, half, drift[0, band, place[c]]
        ).astype(jnp.bfloat16)
    for q in range(secs):
        n, o = window_place(pcol, q, slab)
        n1 = jnp.minimum(n + 1, blocks - 1)
        near, far = (
            corrected(padded, half, i).astype(jnp.bfloat16).astype(jnp.float32) for i in (n, n1)
        )
        picked = jnp.where(lane >= o, near, far)
        acc[q] = pltpu.roll(picked, (BLOCK - o) & (BLOCK - 1), 1)
        notes[owners * CAP * NOTE + 2 * q] = n
        notes[owners * CAP * NOTE + 2 * q + 1] = o
    for k in range(owners):
        source = origin(band, k, owners)
        place, found = find_slots(drift, source, band, drift.shape[2])
        for c in range(CAP):
            goal = drift[2, source, place[c]]
            q = goal // (slab // BLOCK)
            n, o = window_place(pcol, q, slab)
            hit = (found > c) & ((goal == n) | (goal == n + 1))
            at = (k * CAP + c) * NOTE
            notes[at] = jnp.where(hit, 1, 0)
            notes[at + 1] = q
            notes[at + 2] = o
            notes[at + 3] = jnp.where(goal == n, 1, 0)
            notes[at + 4] = drift[0, source, place[c]]
            shares[k * CAP + c] = weight[0, source, place[c]]


def row_differences(x):
    blocks = x.shape[0]
    seg = SEG // BLOCK
    lane = lax.broadcasted_iota(jnp.int32, x.shape, 1)
    block = lax.broadcasted_iota(jnp.int32, x.shape, 0)
    ahead = pltpu.roll(x, BLOCK - 1, 1)
    behind = pltpu.roll(x, 1, 1)
    last_lane = lane == BLOCK - 1
    first_sub = lax.broadcasted_iota(jnp.int32, (SUB, BLOCK), 0) == 0
    first_lane = lane == 0
    nxt = pltpu.roll(ahead, blocks - 1, 0)
    prv = pltpu.roll(behind, 1, 0)
    line = jnp.where(last_lane, jnp.where(block == blocks - 1, 0.0, nxt), ahead) - jnp.where(
        first_lane, jnp.where(block == 0, 0.0, prv), behind
    )
    nxt = jnp.where(block % seg == seg - 1, pltpu.roll(ahead, seg - 1, 0), nxt)
    prv = jnp.where(block % seg == 0, pltpu.roll(behind, blocks - seg + 1, 0), prv)
    ring = jnp.where(last_lane, nxt, ahead) - jnp.where(first_lane, prv, behind)
    return line, ring


def total(x):
    return jnp.sum(jnp.sum(x, axis=1, keepdims=True), axis=0, keepdims=True)


def blend_kernel(owners, secs, notes, shares, jitter_in, edges, begun, *refs):
    messages = refs[:owners]
    jitter_out = refs[owners]
    windows = refs[owners + 1 : owners + 1 + secs]
    firsts, lasts, tails, fixed, acc, den = refs[owners + 1 + secs :]
    blocks = edges.shape[1]
    seg = SEG // BLOCK
    band = lax.axis_index(BANDS)
    sec = lax.axis_index("sec")
    base = CAP * BLOCK
    f32 = jnp.float32
    tiny = 1e-5 * 2 * (blocks // seg)
    firsts[band] = edges[0]
    lasts[band] = edges[1]
    for k in range(1, owners):
        source = origin(band, k, owners)
        firsts[source] = messages[k][base : base + blocks, :].astype(f32)
        lasts[source] = messages[k][base + blocks : base + 2 * blocks, :].astype(f32)
        if messages[k].shape[0] > base + 2 * blocks:
            tails[source] = messages[k][base + 2 * blocks : base + 3 * blocks, :].astype(f32)

    def estimate(row, ring, above):
        return -total(above * ring) / (total(row * row + above * above) + tiny)

    own = jnp.zeros((1, 1), f32)
    for j in range(owners):
        row = firsts[j]
        line, ring = row_differences(row)
        if j == 0:
            fixed[j] = row.astype(jnp.bfloat16).astype(f32)
        else:
            above = lasts[j - 1] + jnp.where(band == j, tails[j - 1], 0.0)
            found = estimate(row, ring, above)
            own = jnp.where(band == j, found, own)
            fixed[j] = (row - 0.5 * found * line).astype(jnp.bfloat16).astype(f32)
    lane_row = lax.broadcasted_iota(jnp.int32, jitter_in.shape, 1)
    jitter_out[...] = jnp.where(lane_row == 0, own, jitter_in[...])

    top = lax.broadcasted_iota(jnp.int32, (BLOCK, BLOCK), 0) == 0
    lane1 = lax.broadcasted_iota(jnp.int32, (1, BLOCK), 1)
    acc[...] = begun[...]
    for q in range(secs):
        n = notes[owners * CAP * NOTE + 2 * q]
        o = notes[owners * CAP * NOTE + 2 * q + 1]
        n1 = jnp.minimum(n + 1, blocks - 1)
        picked = jnp.where(lane1 >= o, fixed[band, pl.ds(n, 1), :], fixed[band, pl.ds(n1, 1), :])
        picked = pltpu.roll(jnp.broadcast_to(picked, (SUB, BLOCK)), (BLOCK - o) & (BLOCK - 1), 1)
        acc[q, 0:1, :] = picked[0:1, :]
        den[q] = jnp.ones((1, BLOCK), f32)

    for k in range(owners):
        source = origin(band, k, owners)
        for c in range(CAP):
            at = (k * CAP + c) * NOTE

            @pl.when(notes[at] > 0)
            def _():
                q, o = notes[at + 1], notes[at + 2]
                w = shares[k * CAP + c]
                turn = (BLOCK - o) & (BLOCK - 1)
                picture = messages[k][c * BLOCK : (c + 1) * BLOCK, :].astype(f32)
                origin_block = notes[at + 4]
                picture = jnp.where(top, fixed[source, pl.ds(origin_block, 1), :], picture)
                inside = (lane1 + o < BLOCK) == (notes[at + 3] > 0)
                factor = jnp.where(inside, w, 0.0)
                acc[q] = acc[q] + factor * pltpu.roll(picture, turn, 1)
                den[q] = den[q] + factor

    for k in range(secs):
        q = target(sec, k, secs)
        windows[k][...] = (acc[q] * (1.0 / den[q])).astype(jnp.bfloat16)


def dot(a, b):
    return jnp.dot(a, b, preferred_element_type=jnp.float32)


def spectra(patches, left, right):
    side = PATCH
    found = []
    for at in range(0, len(patches), 2):
        pair = patches[at : at + 2]
        beside = jnp.concatenate(pair, 1) if len(pair) > 1 else pair[0]
        columns = dot(left, jnp.concatenate([beside, beside], 0))
        stack = []
        for i in range(len(pair)):
            high, low = split(columns[:, i * side : (i + 1) * side])
            stack.append(jnp.concatenate([high, low, high], 1))
        grid = dot(jnp.concatenate(stack, 0), right)
        for i in range(len(pair)):
            one = grid[2 * side * i : 2 * side * (i + 1)]
            real = one[:side, :side] - one[side:, side:]
            imag = -(one[side:, :side] + one[:side, side:])
            found.append((real, imag))
    return found


def spectrum_kernel(left, right, *refs):
    patches, out = refs[:-1], refs[-1]
    for k, (real, imag) in enumerate(spectra([p[...] for p in patches], left[...], right[...])):
        out[k, 0] = real
        out[k, 1] = imag


def surface_kernel(secs, left, right, turn, close, early, *refs):
    late = refs[: secs - early.shape[0]]
    out, freq, held, sent = refs[len(late) :]
    sec = lax.axis_index("sec")
    side = PATCH
    begun = early.shape[0]
    order = patch_order(secs)
    for k in range(begun):
        freq[origin(sec, order[k], secs)] = early[k]
    for k, (real, imag) in enumerate(spectra([p[...] for p in late], left[...], right[...])):
        at = origin(sec, order[begun + k], secs)
        freq[at, 0] = real
        freq[at, 1] = imag
    rows = []
    for s in range(secs - 1):
        real, imag = freq[s, 0], freq[s, 1]
        next_real, next_imag = freq[s + 1, 0], freq[s + 1, 1]
        cross_real = real * next_real + imag * next_imag
        cross_imag = imag * next_real - real * next_imag
        magnitude = jnp.sqrt(cross_real * cross_real + cross_imag * cross_imag)
        damping = (0.5 / (side * side)) * total(magnitude) + 1e-6
        scaled = 1.0 / (magnitude + damping)
        high, low = split(jnp.concatenate([cross_real * scaled, cross_imag * scaled], 1))
        rows.append(jnp.concatenate([high, low, high], 1))
    back = dot(jnp.concatenate(rows, 0), turn[...])
    copies = []
    for s in range(secs - 1):
        one = back[s * side : (s + 1) * side]
        high, low = split(jnp.concatenate([one[:, :side], one[:, side:]], 0))
        held[s] = dot(close[...], jnp.concatenate([high, low, high], 0))
        copies.append(pltpu.make_async_copy(held.at[s], out.at[s], sent.at[s]))
        copies[-1].start()
    for copy in copies:
        copy.wait()


def in_hbm(x):
    return pltpu.with_memory_space_constraint(x, pltpu.HBM)


def in_smem(x):
    return pltpu.with_memory_space_constraint(x, pltpu.SMEM)


def halves(x):
    high = x.astype(jnp.bfloat16)
    return high, (x - high.astype(np.float32)).astype(jnp.bfloat16)


def dft_tables(length):
    indices = np.arange(length)
    angles = (indices[:, None] * indices[None, :] % length) * (2.0 * math.pi / length)
    tables = np.concatenate([np.cos(angles), np.sin(angles)], 1).astype(np.float32)
    return jnp.asarray(np.concatenate(halves(tables), 1))


def fill_tables(tables, left, right, turn, close):
    side = PATCH
    parts = [tables[:, i * side : (i + 1) * side] for i in range(4)]
    for part, (cosine, sine) in enumerate((parts[:2], parts[2:])):
        left[:side, part * side : (part + 1) * side] = cosine
        left[side:, part * side : (part + 1) * side] = sine
        for at in (0, 1) if part == 0 else (2,):
            right[at * side : (at + 1) * side, :side] = cosine
            right[at * side : (at + 1) * side, side:] = sine
            rows = 2 * side * at
            turn[rows : rows + side, :side] = cosine
            turn[rows : rows + side, side:] = sine
            turn[rows + side : rows + 2 * side, :side] = -sine
            turn[rows + side : rows + 2 * side, side:] = cosine
            close[:, rows : rows + side] = cosine * (1.0 / side)
            close[:, rows + side : rows + 2 * side] = -sine * (1.0 / side)


def per_device(section_pixels, jitter_index, drift_list, blend_weight, patch_col):
    pixels = section_pixels[0]
    rows, width = pixels.shape
    blocks = width // BLOCK
    owners = lax.axis_size(BANDS)
    secs = lax.axis_size("sec")
    chunks = len(CHUNKS) - 1
    drifts = jnp.transpose(drift_list[0], (2, 0, 1))
    f32, bf16 = jnp.float32, jnp.bfloat16
    vmem = pl.BlockSpec(memory_space=pltpu.VMEM)
    smem = pl.BlockSpec(memory_space=pltpu.SMEM)
    hbm = pl.BlockSpec(memory_space=pltpu.HBM)
    shape = jax.ShapeDtypeStruct
    message_rows = [
        CAP * BLOCK + (3 if has_tail(k, owners) else 2) * blocks for k in range(1, owners)
    ]
    params = pltpu.CompilerParams(vmem_limit_bytes=24 * 1024 * 1024)
    half, padded, edges, *messages = pl.pallas_call(
        functools.partial(front_kernel, owners),
        out_shape=[
            shape((rows, BLOCK), f32),
            shape((blocks + 2, rows + PAD, BLOCK), f32),
            shape((2, blocks, BLOCK), f32),
        ]
        + [shape((r, BLOCK), bf16) for r in message_rows],
        in_specs=[hbm] * 3,
        out_specs=[vmem] * (2 + owners),
        scratch_shapes=[
            pltpu.VMEM((rows, width), f32),
            pltpu.VMEM((blocks, rows + PAD, BLOCK), f32),
            pltpu.VMEM((rows, rows), jnp.int32),
            pltpu.VMEM((2, rows + SUB, BLOCK), f32),
            pltpu.VMEM((1, rows), jnp.int32),
            pltpu.SMEM(drifts.shape, jnp.int32),
            pltpu.SemaphoreType.DMA((chunks + 2,)),
        ],
        compiler_params=params,
        name="front",
    )(*map(in_hbm, (jitter_index, drifts, pixels)))
    begun, own, notes, shares, left, right, turn, close, jitter = pl.pallas_call(
        functools.partial(plan_kernel, owners, secs),
        out_shape=[
            shape((secs, PATCH, PATCH), f32),
            shape((CAP * BLOCK, BLOCK), bf16),
            pltpu.SMEM((owners * CAP * NOTE + 2 * secs,), jnp.int32),
            pltpu.SMEM((owners * CAP,), f32),
            shape((2 * PATCH, 2 * PATCH), bf16),
            shape((3 * PATCH, 2 * PATCH), bf16),
            shape((6 * PATCH, 2 * PATCH), bf16),
            shape((PATCH, 6 * PATCH), bf16),
            shape((1, rows), f32),
        ],
        in_specs=[hbm] * 4 + [vmem] * 2,
        out_specs=[vmem, vmem, smem, smem] + [vmem] * 5,
        scratch_shapes=[
            pltpu.SMEM(drifts.shape, jnp.int32),
            pltpu.SMEM(blend_weight.shape, f32),
            pltpu.SMEM(patch_col.shape, jnp.int32),
            pltpu.VMEM((PATCH, 4 * PATCH), bf16),
            pltpu.SemaphoreType.DMA((4,)),
        ],
        compiler_params=params,
        cost_estimate=pl.CostEstimate(flops=10**8, bytes_accessed=10**6, transcendentals=0),
        name="plan",
    )(*map(in_hbm, (drifts, blend_weight, patch_col, dft_tables(PATCH))), half, padded)
    messages = [own] + [send(messages[k - 1], BANDS, k, owners) for k in range(1, owners)]
    jitter, *windows = pl.pallas_call(
        functools.partial(blend_kernel, owners, secs),
        out_shape=[shape((1, rows), f32)] + [shape((PATCH, PATCH), bf16)] * secs,
        in_specs=[smem, smem] + [vmem] * (3 + owners),
        out_specs=[vmem] * (1 + secs),
        scratch_shapes=[pltpu.VMEM((owners, blocks, BLOCK), f32)] * 4
        + [pltpu.VMEM((secs, PATCH, PATCH), f32), pltpu.VMEM((secs, 1, PATCH), f32)],
        compiler_params=params,
        name="blend",
    )(in_smem(notes), in_smem(shares), jitter, edges, begun, *messages)
    order = patch_order(secs)
    windows = windows[:1] + [send(windows[k], "sec", k, secs) for k in order[1:]]
    begin = secs // 2
    early = pl.pallas_call(
        spectrum_kernel,
        out_shape=shape((begin, 2, PATCH, PATCH), f32),
        in_specs=[vmem] * (2 + begin),
        out_specs=vmem,
        compiler_params=params,
        cost_estimate=pl.CostEstimate(flops=10**8, bytes_accessed=10**6, transcendentals=0),
        name="spectrum",
    )(left, right, *windows[:begin])
    surfaces = pl.pallas_call(
        functools.partial(surface_kernel, secs),
        out_shape=shape((secs - 1, PATCH, PATCH), f32),
        in_specs=[vmem] * (5 + secs - begin),
        out_specs=hbm,
        scratch_shapes=[
            pltpu.VMEM((secs, 2, PATCH, PATCH), f32),
            pltpu.VMEM((secs - 1, PATCH, PATCH), f32),
            pltpu.SemaphoreType.DMA((secs - 1,)),
        ],
        compiler_params=params,
        name="surface",
    )(left, right, turn, close, early, *windows[begin:])
    return (jitter, surfaces[:, None, None])


def solution(mesh):
    in_specs = (
        P(("groups", "sec"), ("tile", "row"), None),
        P(("groups", "sec"), ("tile", "row")),
        P(("groups", "sec"), None, None, None),
        P(("groups", "sec"), None, None),
        P(("tile", "row"), "groups"),
    )
    out_specs = (
        P(("groups", "sec"), ("tile", "row")),
        P("groups", ("tile", "row"), "sec", None, None),
    )
    return jax.shard_map(
        per_device, mesh=mesh, in_specs=in_specs, out_specs=out_specs, check_vma=False
    )
```
